256 devices in a mesh: group: 8 (over x, core), head: 32 (over y, z).
Axes of the slice: x: 4, y: 4, z: 8, core: 2. Of those that a mesh axis runs over, the one named last changes fastest.
Arguments:
- query_latent: bfloat16 [2048, 1536], P(('group', 'head')), may hold values from -6 to 6
- response_keys: bfloat16 [2048, 576], P(('group', 'head')), may hold values from -8 to 8
- prompt_cache: bfloat16 [256, 147456], P(('group', 'head')), may hold values from -1376 to 1376
- owners: int32 [8], P('group'), may hold values from 0 to 31, as said below
- lengths: int32 [8, 16], P('group'), may hold values from 1 to 16
- w_query_plain: bfloat16 [1536, 16384], P('group', 'head'), may hold values from -0.15625 to 0.15625
- w_query_rotary: bfloat16 [1536, 8192], P('group', 'head'), may hold values from -0.15625 to 0.15625
- w_key_up: bfloat16 [16384, 512], P('head'), may hold values from -0.5 to 0.5
- w_value_up: bfloat16 [512, 16384], P(None, 'head'), may hold values from -0.5 to 0.5
Outputs:
- head_mix: bfloat16 [2048, 16384], P(('group', 'head'))
The draws below stay inside these ranges and needn't reach their ends.
Inputs may be any that keep to these rules, and one draw needn't show every extreme that they name: The 1 group whose tokens lie on one index of group have distinct owners. `lengths`: A response's live tokens are its first ones.
All inputs are finite; a program needn't handle non-finite values.
Results may differ from the reference program's by a relative error of at most 0.024.
Values may be sent and summed in bfloat16 or wider, within the bound.
A program may use at most 192 MiB of HBM per device.

```python
import math
import jax
import jax.numpy as jnp
from jax import lax

LAT = 512
ROPE = 64
NOPE = 128
VDIM = 128
QLAT = 1536
PLEN = 256
G_DEV = 1
RESP = 16
RTOK = 16
HEADS = 128
GROUPS = 8
TOKENS = 2048
SLOTS = 256
N_GROUP = 8
N_HEAD = 32


def draw_owners(key, part):
    key = jax.random.fold_in(key, 5)
    row_seeds = jax.random.split(key, N_GROUP)

    def shuffled(row_seed):
        return jax.random.permutation(row_seed, N_HEAD).astype(jnp.int32)
    orders = jax.vmap(shuffled)(row_seeds)
    first_shift = jnp.argmax(orders[0] == N_HEAD - 1)
    final_shift = jnp.argmax(orders[N_GROUP - 1] == 0)
    orders = orders.at[0].set(jnp.roll(orders[0], -first_shift))
    orders = orders.at[N_GROUP - 1].set(jnp.roll(orders[N_GROUP - 1], -final_shift))
    return orders[:, :G_DEV].reshape(-1).astype(jnp.int32)


def draw_prompt_cache(key, part):
    key = jax.random.fold_in(key, 11)
    latent_seed, rotary_seed = jax.random.split(key, 2)
    latent = jnp.clip(0.7 * jax.random.normal(latent_seed, (SLOTS, PLEN * LAT), jnp.float32), -4.2, 4.2)
    rotary = jnp.clip(jax.random.normal(rotary_seed, (SLOTS, ROPE, PLEN), jnp.float32), -6.0, 6.0)
    return jnp.concatenate([latent, rotary.reshape(SLOTS, ROPE * PLEN)], axis=1).astype(jnp.bfloat16)


def place_ends(drawn, key, least, largest):
    shape = drawn.shape
    spot = [jax.random.randint(jax.random.fold_in(key, axis), (), 0, shape[axis]) for axis in range(len(shape))]
    drawn = drawn.at[tuple(spot)].set(least)
    longest = shape.index(max(shape))
    spot[longest] = (spot[longest] + 1) % shape[longest]
    return drawn.at[tuple(spot)].set(largest)


def steps_of(own_key, shape, shards, smallest, high):
    gain, own = 1.0, jax.random.fold_in(own_key, 6)
    for dim, blocks in shards:
        steps = jnp.exp(jax.random.uniform(jax.random.fold_in(own, dim), (blocks,), jnp.float32, smallest / len(shards), high / len(shards)))
        gain = gain * jnp.repeat(steps, shape[dim] // blocks).reshape([-1 if axis == dim else 1 for axis in range(len(shape))])
    return gain


def bell_draw(rng, extent, spread, bound, shards=(), kind=jnp.bfloat16):
    drawn = spread * jax.random.normal(rng, extent, jnp.float32)
    if shards:
        drawn = drawn * steps_of(rng, extent, shards, -0.22, 0.18)
    return jnp.clip(drawn, -bound, bound).astype(kind)


def setup_inputs(seed: int = 0) -> dict:
    seeds = jax.random.split(jax.random.key(seed), 10)
    return {
        "query_latent": bell_draw(seeds[0], (TOKENS, QLAT), 1.0, 6.0, ((0, 256),)),
        "response_keys": bell_draw(seeds[1], (TOKENS, LAT + ROPE), 1.4, 8.0, ((0, 256),)),
        "prompt_cache": draw_prompt_cache(jax.random.fold_in(seeds[9], 71), 0),
        "owners": draw_owners(jax.random.fold_in(seeds[9], 71), 0),
        "lengths": place_ends(jax.random.randint(seeds[4], (GROUPS, RESP), 1, RTOK + 1), jax.random.fold_in(seeds[4], 1), 1, RTOK).astype(jnp.int32),
        "w_query_plain": bell_draw(seeds[5], (QLAT, HEADS * NOPE), QLAT ** -0.5, 0.15625, ((0, 8), (1, 32))),
        "w_query_rotary": bell_draw(seeds[6], (QLAT, HEADS * ROPE), QLAT ** -0.5, 0.15625, ((0, 8), (1, 32))),
        "w_key_up": bell_draw(seeds[7], (HEADS * NOPE, LAT), NOPE ** -0.5, 0.5, ((0, 32),)),
        "w_value_up": bell_draw(seeds[8], (LAT, HEADS * VDIM), (LAT // 4) ** -0.5, 0.5, ((1, 32),)),
    }


def rotate(values, first_position, period):
    row_count = values.shape[0]
    half_width = values.shape[-1] // 2
    position = (first_position + jnp.arange(row_count) % period).astype(jnp.float32)
    inverse = jnp.exp(jnp.arange(half_width).astype(jnp.float32) * (-2.0 * math.log(10000.0) / values.shape[-1]))
    angle = position[:, None, None] * inverse[None, None, :]
    cosine = jnp.cos(angle)
    sine = jnp.sin(angle)
    former = values[..., :half_width]
    latter = values[..., half_width:]
    return jnp.concatenate([former * cosine - latter * sine, latter * cosine + former * sine], axis=-1)

def narrow(values):
    return lax.optimization_barrier(values.astype(jnp.bfloat16)).astype(jnp.float32)

def reference(query_latent, response_keys, prompt_cache, owners, lengths, w_query_plain, w_query_rotary, w_key_up, w_value_up):
    group_tokens = RESP * RTOK
    scale_factor = 1.0 / math.sqrt(NOPE + ROPE)
    places = jnp.arange(group_tokens)
    within = places % RTOK
    response_of = places // RTOK
    allowed = (response_of[:, None] == response_of[None, :]) & (within[:, None] <= within[None, :])
    key_up = w_key_up.reshape(HEADS, NOPE, LAT).astype(jnp.float32)
    value_up = w_value_up.reshape(LAT, HEADS, VDIM).astype(jnp.float32)

    def one_group(group):
        first_row = (group * group_tokens).astype(jnp.int32)
        rows = lax.dynamic_slice_in_dim(query_latent, first_row, group_tokens, 0)
        fresh = lax.dynamic_slice_in_dim(response_keys, first_row, group_tokens, 0).astype(jnp.float32)
        slot = (group // G_DEV * N_HEAD + owners[group]).astype(jnp.int32)
        cached = lax.dynamic_index_in_dim(prompt_cache, slot, 0, keepdims=False)
        latent = cached[:PLEN * LAT].reshape(PLEN, LAT).astype(jnp.float32)
        rotary = cached[PLEN * LAT:].reshape(ROPE, PLEN).astype(jnp.float32)
        plain = narrow(jnp.dot(rows, w_query_plain, preferred_element_type=jnp.float32)).reshape(group_tokens, HEADS, NOPE)
        turned = jnp.dot(rows, w_query_rotary, preferred_element_type=jnp.float32).reshape(group_tokens, HEADS, ROPE)
        turned = narrow(rotate(turned, PLEN, RTOK))
        absorbed = narrow(jnp.einsum('thn,hnl->htl', plain, key_up))
        prompt_scores = (jnp.einsum('htl,pl->pht', absorbed, latent) + jnp.einsum('thr,rp->pht', turned, rotary)) * scale_factor
        own_scores = (jnp.einsum('htl,sl->sht', absorbed, fresh[:, :LAT]) + jnp.einsum('thr,sr->sht', turned, fresh[:, LAT:])) * scale_factor
        own_masked = jnp.where(allowed[:, None, :], own_scores, -jnp.inf)
        row_top = jnp.maximum(lax.optimization_barrier(jnp.max(prompt_scores, axis=0)), lax.optimization_barrier(jnp.max(own_masked, axis=0)))
        prompt_exp = jnp.exp(prompt_scores - row_top)
        own_exp = jnp.exp(own_masked - row_top)
        denominator = lax.optimization_barrier(jnp.sum(prompt_exp, axis=0)) + lax.optimization_barrier(jnp.sum(own_exp, axis=0))
        prompt_weight = narrow(prompt_exp / denominator)
        own_weight = narrow(own_exp / denominator)
        mixed = jnp.einsum('pht,pl->htl', prompt_weight, latent) + jnp.einsum('sht,sl->htl', own_weight, fresh[:, :LAT])
        mixed = narrow(mixed)
        output = jnp.einsum('htl,lhv->thv', mixed, value_up).reshape(group_tokens, HEADS * VDIM)
        live = (jnp.arange(RTOK)[None, :] < lengths[group][:, None]).reshape(group_tokens)
        return jnp.where(live[:, None], output, 0.0).astype(jnp.bfloat16)
    blocks = lax.map(one_group, jnp.arange(GROUPS, dtype=jnp.int32))
    return blocks.reshape(TOKENS, HEADS * VDIM)
```

```python
import math

import jax
import jax.numpy as jnp
import numpy as np
from jax import lax
from jax.experimental import pallas as pl
from jax.experimental.pallas import tpu as pltpu
from jax.sharding import PartitionSpec as P

MESH = pl.DeviceIdType.MESH
LAT = 512
ROPE = 64
NOPE = 128
VDIM = 128
QLAT = 1536
PLEN = 256
RTOK = 16
TOK = 256
NX, NY, NZ = 4, 4, 8
SHARD = 192
BF = jnp.bfloat16
F32 = jnp.float32
SCALE = 1.0 / math.sqrt(NOPE + ROPE)
LOG2E = 1.4426950408889634


def rotary_tables():
    position = (PLEN + np.arange(TOK) % RTOK).astype(np.float32)
    inverse = np.exp(np.arange(32).astype(np.float32) * np.float32(-2.0 * math.log(10000.0) / ROPE))
    angle = (position[:, None] * inverse[None, :].astype(np.float32)).astype(np.float32)
    cosine, sine = np.cos(angle), np.sin(angle)
    cos_table = np.tile(np.concatenate([cosine, cosine], 1), (1, 4))
    sin_table = np.tile(np.concatenate([-sine, sine], 1), (1, 4))
    return cos_table.astype(np.float32), sin_table.astype(np.float32)


def dot_nt(a, b):
    return lax.dot_general(a, b, (((1,), (1,)), ((), ())), preferred_element_type=F32)


def kernel(
    owner_ref, query_ref, keys_ref, length_ref, cos_ref, sin_ref,
    prompt_hbm, wp_hbm, wr_hbm, ku_hbm, vu_hbm,
    out_ref,
    wp, wr, ku, vu, flat, stage, q_send, k_send, qb, kb,
    p_send, r_send, p_recv, r_recv, z_send, z_recv, pl_buf,
    x_buf, fresh, fresh_rot, latent, rotary, plain, turned, absorbed, o_send,
    local_sem, wx_send, wx_recv, wc_send, wc_recv,
    qz_send, qz_recv, qy_send, qy_recv, ky_send, ky_recv, kz_send, kz_recv,
    pa_send, pa_recv, pz_send, pz_recv, pg_send, pg_recv, py_send, py_recv,
    o_ssem, o_rsem,
):
    g = lax.axis_index("group")
    h = lax.axis_index("head")
    x, c = g // 2, g % 2
    y, z = h // NZ, h % NZ

    def at_x(d):
        return (lax.rem(x + d, NX) * 2 + c, h)

    def at_y(d):
        return (g, lax.rem(y + d, NY) * NZ + z)

    def at_z(d):
        return (g, y * NZ + lax.rem(z + d, NZ))

    sibling = (x * 2 + 1 - c, h)

    def remote(src, dst, ssem, rsem, device):
        return pltpu.make_async_remote_copy(src, dst, ssem, rsem, device_id=device, device_id_type=MESH)

    barrier = pltpu.get_barrier_semaphore()
    peers = [sibling] + [at_x(d) for d in (1, 2, 3)] + [at_y(d) for d in (1, 2, 3)] + [at_z(d) for d in range(1, 8)]
    for peer in peers:
        pl.semaphore_signal(barrier, inc=1, device_id=peer, device_id_type=MESH)

    mine = pl.ds(pl.multiple_of(g * SHARD, 64), SHARD)
    flat_copy = pltpu.make_async_copy(prompt_hbm, flat, local_sem.at[0])
    flat_copy.start()
    ku_copy = pltpu.make_async_copy(ku_hbm, ku, local_sem.at[1])
    vu_copy = pltpu.make_async_copy(vu_hbm, vu, local_sem.at[2])
    wp_copy = pltpu.make_async_copy(wp_hbm, wp.at[mine], local_sem.at[3])
    wr_copy = pltpu.make_async_copy(wr_hbm, wr.at[mine], local_sem.at[4])
    for copy in (wp_copy, wr_copy, ku_copy, vu_copy):
        copy.start()

    query = query_ref[...].astype(F32)
    packed = jnp.concatenate([query[:, :768], query[:, 768:]], axis=0).astype(BF)
    q_send[...] = packed
    qb[pl.ds(h, 1)] = packed[None]
    keys = keys_ref[...].astype(F32)
    tail = jnp.concatenate([keys[:, 512:], jnp.zeros((8, 64), F32)], axis=1)
    packed = jnp.concatenate(
        [
            jnp.concatenate([keys[:, :256], tail], axis=1),
            jnp.concatenate([keys[:, 256:512], jnp.zeros((8, 128), F32)], axis=1),
        ],
        axis=0,
    ).astype(BF)
    k_send[...] = packed
    kb[pl.ds(y, 1), pl.ds(z, 1)] = packed[None, None]

    pl.semaphore_wait(barrier, len(peers))

    w_out = []
    for d in (1, 3, 2):
        w_out.append(remote(wp_hbm, wp.at[mine], wx_send.at[d, 0], wx_recv.at[d, 0], at_x(d)))
        w_out.append(remote(wr_hbm, wr.at[mine], wx_send.at[d, 1], wx_recv.at[d, 1], at_x(d)))
    w_out.append(remote(wp_hbm, wp.at[mine], wc_send.at[0, 0], wc_recv.at[0, 0], sibling))
    w_out.append(remote(wr_hbm, wr.at[mine], wc_send.at[0, 1], wc_recv.at[0, 1], sibling))
    k_out = [remote(k_send, kb.at[y, z], ky_send.at[d], ky_recv.at[d], at_y(d)) for d in (1, 3, 2)]
    q_out = [remote(q_send, qb.at[h], qz_send.at[d], qz_recv.at[d], at_z(d)) for d in (4, 3, 5, 2, 6, 1, 7)]
    for copy in k_out + q_out + w_out:
        copy.start()

    flat_copy.wait()

    @pl.loop(0, PLEN // 8)
    def _(block):
        for r in range(8):
            row = flat[0:1, pl.ds(pl.multiple_of(block * 4096 + r * 512, 512), 512)].astype(F32)
            stage[pl.ds(block * 8 + r, 1), :] = row
        both = stage[pl.ds(pl.multiple_of(block * 8, 8), 8), :]
        p_send[pl.ds(block // 8, 1), pl.ds(block % 8, 1)] = jnp.concatenate(
            [both[:, :256], both[:, 256:]], axis=0
        ).astype(BF)[None, None]

    @pl.loop(0, NY)
    def _(j):
        for r in range(16):
            row = flat[0:1, pl.ds(pl.multiple_of(PLEN * LAT + j * 4096 + r * 256, 256), 256)].astype(F32)
            stage[pl.ds(r, 1), 0:256] = row
        both = stage[0:16, 0:256].astype(BF)
        r_send[pl.ds(j, 1), 0:1] = both[None, None, :, :128]
        r_send[pl.ds(j, 1), 1:2] = both[None, None, :, 128:]

    p_out = []
    for d in (1, 3, 2):
        there = lax.rem(y + d, NY)
        p_out.append(remote(p_send.at[there], p_recv.at[y], pa_send.at[d, 0], pa_recv.at[d, 0], at_y(d)))
        p_out.append(remote(r_send.at[there], r_recv.at[y], pa_send.at[d, 1], pa_recv.at[d, 1], at_y(d)))
    for copy in p_out:
        copy.start()
    p_recv[pl.ds(y, 1)] = p_send[pl.ds(y, 1)]
    r_recv[pl.ds(y, 1)] = r_send[pl.ds(y, 1)]

    for copy in k_out:
        copy.wait_recv()
    kz_out = [remote(kb.at[:, z], kb.at[:, z], kz_send.at[d], kz_recv.at[d], at_z(d)) for d in (4, 3, 5, 2, 6, 1, 7)]

    for copy in q_out:
        copy.wait_recv()
    row = pl.ds(pl.multiple_of(y * NZ, NZ), NZ)
    qy_out = [remote(qb.at[row], qb.at[row], qy_send.at[d], qy_recv.at[d], at_y(d)) for d in (1, 3, 2)]
    for copy in qy_out + kz_out:
        copy.start()

    owner = owner_ref[0]
    for copy in p_out:
        copy.wait_recv()
    chosen = p_recv[owner // NZ]
    chosen_rot = r_recv[owner // NZ]
    for k in range(NZ):
        z_send[k] = jnp.concatenate([chosen[k], chosen_rot[k % 2]], axis=1)
    pz_out = []
    for d in (4, 3, 5, 2, 6, 1, 7):
        pz_out.append(remote(z_send.at[lax.rem(z + d, NZ)], z_recv.at[z], pz_send.at[d], pz_recv.at[d], at_z(d)))
    for copy in pz_out:
        copy.start()
    z_recv[pl.ds(z, 1)] = z_send[pl.ds(z, 1)]

    wc_out = []

    def pass_on(d):
        there = pl.ds(pl.multiple_of((lax.rem(x + NX - d, NX) * 2 + c) * SHARD, 64), SHARD)
        for i, ref in enumerate((wp, wr)):
            pltpu.make_async_remote_copy(
                ref.at[there], ref.at[there], wx_send.at[d, i], wx_recv.at[d, i], device_id=at_x(d), device_id_type=MESH
            ).wait_recv()
            wc_out.append(remote(ref.at[there], ref.at[there], wc_send.at[d, i], wc_recv.at[d, i], sibling))
            wc_out[-1].start()

    pass_on(1)
    pass_on(3)

    for copy in pz_out:
        copy.wait_recv()
    pl_buf[pl.ds(y, 1), pl.ds(z, 1)] = z_recv[owner % NZ][None, None]
    pg_out = [remote(pl_buf.at[y, z], pl_buf.at[y, z], pg_send.at[d], pg_recv.at[d], at_z(d)) for d in (4, 3, 5, 2, 6, 1, 7)]
    for copy in pg_out:
        copy.start()
    pass_on(2)
    for copy in pg_out:
        copy.wait_recv()
    py_out = []
    for d in (1, 3, 2):
        part = pl_buf.at[y, :, :, 0:256]
        py_out.append(remote(part, part, py_send.at[d, 0], py_recv.at[d, 0], at_y(d)))
        part = pl_buf.at[y, 0:2, :, 256:384]
        py_out.append(remote(part, part, py_send.at[d, 1], py_recv.at[d, 1], at_y(d)))
    for copy in py_out:
        copy.start()

    for copy in qy_out:
        copy.wait_recv()
    gathered = qb[...].astype(F32)
    x_buf[:, :768] = gathered[:, :8].reshape(TOK, 768).astype(BF)
    x_buf[:, 768:] = gathered[:, 8:].reshape(TOK, 768).astype(BF)
    wp_copy.wait()
    wr_copy.wait()
    for d in range(NX):
        there = pl.ds(pl.multiple_of((lax.rem(x + NX - d, NX) * 2 + 1 - c) * SHARD, 64), SHARD)
        for i, ref in enumerate((wp, wr)):
            remote(ref.at[there], ref.at[there], wc_send.at[d, i], wc_recv.at[d, i], sibling).wait_recv()
    rows = x_buf[...]
    plain[...] = jnp.dot(rows, wp[...], preferred_element_type=F32).astype(BF)
    spun = jnp.dot(rows, wr[...], preferred_element_type=F32)
    lane = lax.broadcasted_iota(jnp.int32, (TOK, 256), 1)
    swapped = jnp.where(lane % 64 < 32, pltpu.roll(spun, 224, 1), pltpu.roll(spun, 32, 1))
    turned[...] = (spun * cos_ref[...] + swapped * sin_ref[...]).astype(BF)

    ku_copy.wait()
    for i in range(4):
        absorbed[i] = jnp.dot(
            plain[:, i * 128 : (i + 1) * 128], ku[i * 128 : (i + 1) * 128, :], preferred_element_type=F32
        ).astype(BF)

    for copy in kz_out:
        copy.wait_recv()
    gathered = kb[...].astype(F32).reshape(32, 16, 384)
    fresh[:, :256] = gathered[:, :8, :256].reshape(TOK, 256).astype(BF)
    fresh[:, 256:] = gathered[:, 8:, :256].reshape(TOK, 256).astype(BF)
    rot = gathered[:, :8, 256:].reshape(TOK, 128)
    fresh_rot[...] = (rot + pltpu.roll(rot, 64, 1)).astype(BF)

    lengths = jnp.broadcast_to(length_ref[...], (TOK, 16))
    token = lax.broadcasted_iota(jnp.int32, (TOK, 16), 0)
    slot = lax.broadcasted_iota(jnp.int32, (TOK, 16), 1)
    limit = jnp.sum(jnp.where(token // RTOK == slot, lengths, 0).astype(F32), axis=1, keepdims=True)
    place = (lax.broadcasted_iota(jnp.int32, (TOK, 1), 0) % RTOK).astype(F32)
    live = place < limit

    t_half = lax.broadcasted_iota(jnp.int32, (128, 128), 0)
    s_half = lax.broadcasted_iota(jnp.int32, (128, 128), 1)
    allowed = (t_half // RTOK == s_half // RTOK) & (s_half <= t_half)
    pair_lane = lax.broadcasted_iota(jnp.int32, (TOK, 128), 1)

    for copy in py_out:
        copy.wait_recv()
    gathered = pl_buf[:, :, :, :256].astype(F32).reshape(32, 16, 256)
    latent[:, :256] = gathered[:, :8].reshape(PLEN, 256).astype(BF)
    latent[:, 256:] = gathered[:, 8:].reshape(PLEN, 256).astype(BF)
    for j in range(NY):
        both = jnp.concatenate([pl_buf[j, 0, :, 256:], pl_buf[j, 1, :, 256:]], axis=1)
        rotary[j * 16 : (j + 1) * 16, :] = both
        rotary[64 + j * 16 : 64 + (j + 1) * 16, :] = both
    vu_copy.wait()

    for pair in range(2):
        outs = []
        pair_turned = turned[:, pair * 128 : (pair + 1) * 128]
        for sub in range(2):
            i = pair * 2 + sub
            a = absorbed[i]
            mine_lanes = (pair_lane < 64) if sub == 0 else (pair_lane >= 64)
            t = jnp.where(mine_lanes, pair_turned.astype(F32), 0.0).astype(BF)
            prompt_scores = dot_nt(a, latent[...]) + jnp.dot(t, rotary[...], preferred_element_type=F32)
            own = []
            for half in range(2):
                part = slice(half * 128, (half + 1) * 128)
                scores = dot_nt(a[part], fresh[part, :]) + dot_nt(t[part], fresh_rot[part, :])
                own.append(jnp.where(allowed, scores, -jnp.inf))
            own_scores = jnp.concatenate(own, axis=0)
            top = jnp.max(
                jnp.maximum(jnp.maximum(prompt_scores[:, :128], prompt_scores[:, 128:]), own_scores),
                axis=1,
                keepdims=True,
            )
            prompt_exp = jnp.exp2((prompt_scores - top) * (SCALE * LOG2E))
            own_exp = jnp.exp2((own_scores - top) * (SCALE * LOG2E))
            total = jnp.sum(prompt_exp[:, :128] + prompt_exp[:, 128:] + own_exp, axis=1, keepdims=True)
            factor = jnp.where(live, 1.0 / total, 0.0)
            own_weight = own_exp.astype(BF)
            mixed = jnp.dot(prompt_exp.astype(BF), latent[...], preferred_element_type=F32)
            mixed_own = jnp.concatenate(
                [
                    jnp.dot(own_weight[:128], fresh[:128, :], preferred_element_type=F32),
                    jnp.dot(own_weight[128:], fresh[128:, :], preferred_element_type=F32),
                ],
                axis=0,
            )
            mixed = ((mixed + mixed_own) * factor).astype(BF)
            out = jnp.dot(mixed, vu[:, i * 128 : (i + 1) * 128], preferred_element_type=F32)
            outs.append(out.reshape(32, 8, 128))
        o_send[pair] = jnp.concatenate(outs, axis=1).astype(BF)

        @pl.loop(1, 32)
        def _(d):
            there = lax.rem(h + d, 32)
            remote(o_send.at[pair, there], out_ref.at[pair, h], o_ssem.at[pair], o_rsem.at[pair], (g, there)).start()

        keep = pltpu.make_async_copy(o_send.at[pair, h], out_ref.at[pair, h], local_sem.at[5 + pair])
        keep.start()

    for copy in w_out + wc_out + k_out + q_out + qy_out + kz_out + p_out + pz_out + pg_out + py_out:
        copy.wait_send()
    for pair in range(2):
        pltpu.make_async_copy(o_send.at[pair, h], out_ref.at[pair, h], local_sem.at[5 + pair]).wait()
        whole = remote(
            o_send.at[pair, pl.ds(0, 31)], out_ref.at[pair, pl.ds(0, 31)], o_ssem.at[pair], o_rsem.at[pair], sibling
        )
        whole.wait_send()
        whole.wait_recv()


def local(
    query_latent, response_keys, prompt_cache, owners, lengths, w_query_plain, w_query_rotary, w_key_up, w_value_up
):
    cos_table, sin_table = rotary_tables()
    vmem = pl.BlockSpec(memory_space=pltpu.VMEM)
    smem = pl.BlockSpec(memory_space=pltpu.SMEM)
    hbm = pl.BlockSpec(memory_space=pl.ANY)
    dma = pltpu.SemaphoreType.DMA
    gathered = pl.pallas_call(
        kernel,
        out_shape=jax.ShapeDtypeStruct((2, 32, 16, 128), BF),
        in_specs=[smem, vmem, vmem, vmem, vmem, vmem, hbm, hbm, hbm, hbm, hbm],
        out_specs=vmem,
        scratch_shapes=[
            pltpu.VMEM((QLAT, 512), BF),
            pltpu.VMEM((QLAT, 256), BF),
            pltpu.VMEM((512, 512), BF),
            pltpu.VMEM((512, 512), BF),
            pltpu.VMEM((1, 147456), BF),
            pltpu.VMEM((PLEN, 512), F32),
            pltpu.VMEM((16, 768), BF),
            pltpu.VMEM((16, 384), BF),
            pltpu.VMEM((32, 16, 768), BF),
            pltpu.VMEM((NY, NZ, 16, 384), BF),
            pltpu.VMEM((NY, NZ, 16, 256), BF),
            pltpu.VMEM((NY, 2, 16, 128), BF),
            pltpu.VMEM((NY, NZ, 16, 256), BF),
            pltpu.VMEM((NY, 2, 16, 128), BF),
            pltpu.VMEM((NZ, 16, 384), BF),
            pltpu.VMEM((NZ, 16, 384), BF),
            pltpu.VMEM((NY, NZ, 16, 384), BF),
            pltpu.VMEM((TOK, QLAT), BF),
            pltpu.VMEM((TOK, 512), BF),
            pltpu.VMEM((TOK, 128), BF),
            pltpu.VMEM((PLEN, 512), BF),
            pltpu.VMEM((128, PLEN), BF),
            pltpu.VMEM((TOK, 512), BF),
            pltpu.VMEM((TOK, 256), BF),
            pltpu.VMEM((4, TOK, 512), BF),
            pltpu.VMEM((2, 32, 16, 128), BF),
            dma((7,)),
            dma((4, 2)),
            dma((4, 2)),
            dma((4, 2)),
            dma((4, 2)),
            dma((8,)),
            dma((8,)),
            dma((4,)),
            dma((4,)),
            dma((4,)),
            dma((4,)),
            dma((8,)),
            dma((8,)),
            dma((4, 2)),
            dma((4, 2)),
            dma((8,)),
            dma((8,)),
            dma((8,)),
            dma((8,)),
            dma((4, 2)),
            dma((4, 2)),
            dma((2,)),
            dma((2,)),
        ],
        compiler_params=pltpu.CompilerParams(collective_id=0, has_side_effects=True, vmem_limit_bytes=40 << 20),
    )(
        owners,
        query_latent,
        response_keys,
        lengths,
        jnp.asarray(cos_table),
        jnp.asarray(sin_table),
        prompt_cache,
        w_query_plain,
        w_query_rotary,
        w_key_up,
        w_value_up,
    )
    return gathered.reshape(2, 32, 2, 8, 128).transpose(3, 1, 0, 2, 4).reshape(8, 16384)


def solution(mesh):
    return jax.shard_map(
        local,
        mesh=mesh,
        in_specs=(
            P(("group", "head"), None),
            P(("group", "head"), None),
            P(("group", "head"), None),
            P("group"),
            P("group", None),
            P("group", "head"),
            P("group", "head"),
            P("head", None),
            P(None, "head"),
        ),
        out_specs=P(("group", "head"), None),
        check_vma=False,
    )
```

```python
import math

import jax
import jax.numpy as jnp
import numpy as np
from jax import lax
from jax.experimental import pallas as pl
from jax.experimental.pallas import tpu as pltpu
from jax.sharding import PartitionSpec as P

MESH = pl.DeviceIdType.MESH
LAT = 512
ROPE = 64
NOPE = 128
VDIM = 128
QLAT = 1536
PLEN = 256
RTOK = 16
TOK = 256
NX, NY, NZ = 4, 4, 8
SHARD = 192
HALF = 96
BF = jnp.bfloat16
F32 = jnp.float32
SCALE = 1.0 / math.sqrt(NOPE + ROPE)
LOG2E = 1.4426950408889634


def rotary_tables():
    position = (PLEN + np.arange(RTOK)).astype(np.float32)
    inverse = np.exp(np.arange(32).astype(np.float32) * np.float32(-2.0 * math.log(10000.0) / ROPE))
    angle = (position[:, None] * inverse[None, :].astype(np.float32)).astype(np.float32)
    cosine, sine = np.cos(angle), np.sin(angle)
    cos_table = np.tile(np.concatenate([cosine, cosine], 1), (1, 4))
    sin_table = np.tile(np.concatenate([-sine, sine], 1), (1, 4))
    return np.concatenate([cos_table, sin_table], 0).astype(np.float32)


def dot_nt(a, b):
    return lax.dot_general(a, b, (((1,), (1,)), ((), ())), preferred_element_type=F32)


def kernel(
    owner_hbm, query_hbm, keys_hbm, length_hbm, table_hbm, prompt_hbm, wp_hbm, wr_hbm, ku_hbm, vu_hbm,
    out_ref,
    owner_ref, query_ref, keys_ref, length_ref, table_ref, w, ku, vu, flat, stage, q_send, k_send, r_own, qb, kl, kt, kr,
    p_send, r_send, p_recv, r_recv, z_send, z_recv, pl_buf,
    x_buf, fresh, fresh_rot, latent, rotary, plain, turned, absorbed, own_buf, o_send,
    local_sem, wx_send, wx_recv, wf_send, wf_recv, wc_send, wc_recv,
    qz_send, qz_recv, qy_send, qy_recv, ky_send, ky_recv, kz_send, kz_recv,
    pa_send, pa_recv, pz_send, pz_recv, pg_send, pg_recv, py_send, py_recv,
    o_ssem, o_rsem,
):
    g = lax.axis_index("group")
    h = lax.axis_index("head")
    x, c = g // 2, g % 2
    y, z = h // NZ, h % NZ

    def at_x(d):
        return (lax.rem(x + d, NX) * 2 + c, h)

    def at_y(d):
        return (g, lax.rem(y + d, NY) * NZ + z)

    def at_z(d):
        return (g, y * NZ + lax.rem(z + d, NZ))

    sibling = (x * 2 + 1 - c, h)
    y_order = (1, 3, 2)
    z_order = (4, 3, 5, 2, 6, 1, 7)

    def remote(src, dst, ssem, rsem, device):
        return pltpu.make_async_remote_copy(src, dst, ssem, rsem, device_id=device, device_id_type=MESH)

    barrier = pltpu.get_barrier_semaphore()
    peers = [sibling] + [at_x(d) for d in (1, 3)] + [at_y(d) for d in y_order] + [at_z(d) for d in z_order]
    for peer in peers:
        pl.semaphore_signal(barrier, inc=1, device_id=peer, device_id_type=MESH)

    def half_rows(dx, core, half):
        start = (lax.rem(x + dx + NX, NX) * 2 + core) * SHARD + half * HALF
        return pl.ds(pl.multiple_of(start, 32), HALF)

    mine = pl.ds(pl.multiple_of(g * SHARD, 64), SHARD)
    flat_copy = pltpu.make_async_copy(prompt_hbm, flat, local_sem.at[0])
    query_copy = pltpu.make_async_copy(query_hbm, query_ref, local_sem.at[7])
    keys_copy = pltpu.make_async_copy(keys_hbm, keys_ref, local_sem.at[8])
    wp_copy = pltpu.make_async_copy(wp_hbm, w.at[mine, 0:512], local_sem.at[3])
    wr_copy = pltpu.make_async_copy(wr_hbm, w.at[mine, 512:768], local_sem.at[4])
    owner_copy = pltpu.make_async_copy(owner_hbm, owner_ref, local_sem.at[9])
    length_copy = pltpu.make_async_copy(length_hbm, length_ref, local_sem.at[10])
    table_copy = pltpu.make_async_copy(table_hbm, table_ref, local_sem.at[11])
    ku_copy = pltpu.make_async_copy(ku_hbm, ku, local_sem.at[1])
    vu_copy = pltpu.make_async_copy(vu_hbm, vu, local_sem.at[2])
    for copy in (
        flat_copy, query_copy, keys_copy, wp_copy, wr_copy, owner_copy, length_copy, table_copy, ku_copy, vu_copy
    ):
        copy.start()

    flat_copy.wait()

    @pl.loop(0, PLEN // 8)
    def _(block):
        for r in range(8):
            row = flat[0:1, pl.ds(pl.multiple_of(block * 4096 + r * 512, 512), 512)].astype(F32)
            stage[pl.ds(block * 8 + r, 1), :] = row
        both = stage[pl.ds(pl.multiple_of(block * 8, 8), 8), :]
        p_send[pl.ds(block // 8, 1), pl.ds(block % 8, 1)] = jnp.concatenate(
            [both[:, :256], both[:, 256:]], axis=0
        ).astype(BF)[None, None]

    @pl.loop(0, NY)
    def _(j):
        for r in range(16):
            row = flat[0:1, pl.ds(pl.multiple_of(PLEN * LAT + j * 4096 + r * 256, 256), 256)].astype(F32)
            stage[pl.ds(r, 1), 0:256] = row
        both = stage[0:16, 0:256].astype(BF)
        r_send[pl.ds(j, 1), 0:1] = both[None, None, :, :128]
        r_send[pl.ds(j, 1), 1:2] = both[None, None, :, 128:]

    p_recv[pl.ds(y, 1)] = p_send[pl.ds(y, 1)]
    r_recv[pl.ds(y, 1)] = r_send[pl.ds(y, 1)]

    query_copy.wait()
    query = query_ref[...].astype(F32)
    packed = jnp.concatenate([query[:, :768], query[:, 768:]], axis=0).astype(BF)
    q_send[...] = packed
    qb[pl.ds(h, 1)] = packed[None]
    keys_copy.wait()
    keys = keys_ref[...].astype(F32)
    packed = jnp.concatenate([keys[:, :256], keys[:, 256:512]], axis=0).astype(BF)
    k_send[...] = packed
    kl[pl.ds(y, 1), pl.ds(z, 1)] = packed[None, None]
    rot = jnp.concatenate([keys[:, 512:], keys[:, 512:]], axis=1)
    packed = jnp.concatenate([rot, rot], axis=0).astype(BF)
    r_own[...] = packed
    kt[pl.ds(y, 1)] = packed[None]
    wp_copy.wait()
    wr_copy.wait()

    pl.semaphore_wait(barrier, len(peers))

    p_out, k_out = [], []
    for d in y_order:
        there = lax.rem(y + d, NY)
        k_out.append(remote(k_send, kl.at[y, z], ky_send.at[d, 0], ky_recv.at[d, 0], at_y(d)))
        k_out.append(remote(r_own, kt.at[y], ky_send.at[d, 1], ky_recv.at[d, 1], at_y(d)))
        p_out.append(remote(p_send.at[there], p_recv.at[y], pa_send.at[d, 0], pa_recv.at[d, 0], at_y(d)))
        p_out.append(remote(r_send.at[there], r_recv.at[y], pa_send.at[d, 1], pa_recv.at[d, 1], at_y(d)))
    q_out = [remote(q_send, qb.at[h], qz_send.at[d], qz_recv.at[d], at_z(d)) for d in z_order]
    w_out = []
    for step in range(2):
        for d in (1, 3):
            half = step if d == 1 else 1 - step
            rows = w.at[half_rows(0, c, half)]
            w_out.append(remote(rows, rows, wx_send.at[d, half], wx_recv.at[d, half], at_x(d)))
    for copy in p_out + k_out + q_out + w_out:
        copy.start()
    wc_out = []

    def to_sibling(dx, half):
        rows = w.at[half_rows(dx, c, half)]
        wc_out.append(remote(rows, rows, wc_send.at[dx, half], wc_recv.at[dx, half], sibling))
        wc_out[-1].start()

    def from_sibling(dx, half):
        rows = w.at[half_rows(dx, 1 - c, half)]
        remote(rows, rows, wc_send.at[dx, half], wc_recv.at[dx, half], sibling).wait_recv()

    def arrived(d, half):
        rows = w.at[half_rows(NX - d, c, half)]
        remote(rows, rows, wx_send.at[d, half], wx_recv.at[d, half], at_x(d)).wait_recv()

    to_sibling(0, 0)
    to_sibling(0, 1)

    for copy in k_out:
        copy.wait_recv()
    tiles = kt[...].astype(F32)
    tile_row = lax.broadcasted_iota(jnp.int32, (16, 128), 0)
    tile_lane = lax.broadcasted_iota(jnp.int32, (16, 128), 1)
    upper = jnp.where(tile_lane < 64, tiles[0], tiles[1])
    lower = jnp.where(tile_lane < 64, tiles[2], tiles[3])
    kr[pl.ds(z, 1)] = jnp.where(tile_row < 8, upper, lower).astype(BF)[None]
    kz_out = []
    for d in z_order:
        kz_out.append(remote(kl.at[:, z], kl.at[:, z], kz_send.at[d, 0], kz_recv.at[d, 0], at_z(d)))
        kz_out.append(remote(kr.at[z], kr.at[z], kz_send.at[d, 1], kz_recv.at[d, 1], at_z(d)))

    wf_out = []

    def pass_on(d, half):
        arrived(d, half)
        rows = w.at[half_rows(NX - d, c, half)]
        wf_out.append(remote(rows, rows, wf_send.at[half], wf_recv.at[half], at_x(d)))
        wf_out[-1].start()
        to_sibling(NX - d, half)

    pass_on(1, 0)
    pass_on(3, 1)

    owner_copy.wait()
    owner = owner_ref[0]
    for copy in p_out:
        copy.wait_recv()
    chosen = p_recv[owner // NZ]
    chosen_rot = r_recv[owner // NZ]
    for k in range(NZ):
        z_send[k] = jnp.concatenate([chosen[k], chosen_rot[k % 2]], axis=1)
    pz_out = []
    for d in z_order:
        pz_out.append(remote(z_send.at[lax.rem(z + d, NZ)], z_recv.at[z], pz_send.at[d], pz_recv.at[d], at_z(d)))
    for copy in pz_out:
        copy.start()
    z_recv[pl.ds(z, 1)] = z_send[pl.ds(z, 1)]

    for copy in q_out:
        copy.wait_recv()
    row = pl.ds(pl.multiple_of(y * NZ, NZ), NZ)
    qy_out = [remote(qb.at[row], qb.at[row], qy_send.at[d], qy_recv.at[d], at_y(d)) for d in y_order]
    for copy in qy_out + kz_out:
        copy.start()

    for copy in pz_out:
        copy.wait_recv()
    pl_buf[pl.ds(y, 1), pl.ds(z, 1)] = z_recv[owner % NZ][None, None]
    pg_out = [remote(pl_buf.at[y, z], pl_buf.at[y, z], pg_send.at[d], pg_recv.at[d], at_z(d)) for d in z_order]
    for copy in pg_out:
        copy.start()

    arrived(1, 1)
    to_sibling(3, 1)
    arrived(3, 0)
    to_sibling(1, 0)
    for half in range(2):
        rows = w.at[half_rows(2, c, half)]
        remote(rows, rows, wf_send.at[half], wf_recv.at[half], sibling).wait_recv()
        to_sibling(2, half)

    for copy in pg_out:
        copy.wait_recv()
    py_out = []
    for d in y_order:
        part = pl_buf.at[y, :, :, 0:256]
        py_out.append(remote(part, part, py_send.at[d, 0], py_recv.at[d, 0], at_y(d)))
        part = pl_buf.at[y, 0:2, :, 256:384]
        py_out.append(remote(part, part, py_send.at[d, 1], py_recv.at[d, 1], at_y(d)))
    for copy in py_out:
        copy.start()

    for copy in qy_out:
        copy.wait_recv()
    gathered = qb[...].astype(F32)
    x_buf[:, :768] = gathered[:, :8].reshape(TOK, 768).astype(BF)
    x_buf[:, 768:] = gathered[:, 8:].reshape(TOK, 768).astype(BF)
    for dx in range(NX):
        for half in range(2):
            from_sibling(dx, half)
    both = jnp.dot(x_buf[...], w[...], preferred_element_type=F32)
    plain[...] = both[:, :512].astype(BF)
    spun = both[:, 512:]
    lane = lax.broadcasted_iota(jnp.int32, (TOK, 256), 1)
    swapped = jnp.where(lane % 64 < 32, pltpu.roll(spun, 224, 1), pltpu.roll(spun, 32, 1))
    table_copy.wait()
    cosine = jnp.broadcast_to(table_ref[:16][None], (16, 16, 256)).reshape(TOK, 256)
    sine = jnp.broadcast_to(table_ref[16:][None], (16, 16, 256)).reshape(TOK, 256)
    turned[...] = (spun * cosine + swapped * sine).astype(BF)

    ku_copy.wait()
    for i in range(4):
        absorbed[i] = jnp.dot(
            plain[:, i * 128 : (i + 1) * 128], ku[i * 128 : (i + 1) * 128, :], preferred_element_type=F32
        ).astype(BF)

    for copy in kz_out:
        copy.wait_recv()
    gathered = kl[...].astype(F32).reshape(32, 16, 256)
    fresh[:, :256] = gathered[:, :8].reshape(TOK, 256).astype(BF)
    fresh[:, 256:] = gathered[:, 8:].reshape(TOK, 256).astype(BF)
    gathered = kr[...].astype(F32)
    rot_lane = lax.broadcasted_iota(jnp.int32, (64, 128), 1)
    for j in range(NY):
        piece = gathered[:, (j // 2) * 8 : (j // 2) * 8 + 8].reshape(64, 128)
        piece = jnp.where((rot_lane < 64) if j % 2 == 0 else (rot_lane >= 64), piece, 0.0)
        fresh_rot[j * 64 : (j + 1) * 64, :] = (piece + pltpu.roll(piece, 64, 1)).astype(BF)

    length_copy.wait()
    lengths = jnp.broadcast_to(length_ref[...], (TOK, 16))
    token = lax.broadcasted_iota(jnp.int32, (TOK, 16), 0)
    slot = lax.broadcasted_iota(jnp.int32, (TOK, 16), 1)
    limit = jnp.sum(jnp.where(token // RTOK == slot, lengths, 0).astype(F32), axis=1, keepdims=True)
    place = (lax.broadcasted_iota(jnp.int32, (TOK, 1), 0) % RTOK).astype(F32)
    live = place < limit

    t_half = lax.broadcasted_iota(jnp.int32, (128, 128), 0)
    s_half = lax.broadcasted_iota(jnp.int32, (128, 128), 1)
    allowed = (t_half // RTOK == s_half // RTOK) & (s_half <= t_half)
    pair_lane = lax.broadcasted_iota(jnp.int32, (TOK, 128), 1)

    def own_turned(i):
        mine_lanes = (pair_lane < 64) if i % 2 == 0 else (pair_lane >= 64)
        part = turned[:, (i // 2) * 128 : (i // 2 + 1) * 128].astype(F32)
        return jnp.where(mine_lanes, part, 0.0).astype(BF)

    for i in range(4):
        t = own_turned(i)
        for half in range(2):
            part = slice(half * 128, (half + 1) * 128)
            scores = dot_nt(absorbed[i, part, :], fresh[part, :]) + dot_nt(t[part], fresh_rot[part, :])
            own_buf[i, part, :] = jnp.where(allowed, scores, -jnp.inf)
    vu_copy.wait()

    for copy in py_out:
        copy.wait_recv()
    gathered = pl_buf[:, :, :, :256].astype(F32).reshape(32, 16, 256)
    latent[:, :256] = gathered[:, :8].reshape(PLEN, 256).astype(BF)
    latent[:, 256:] = gathered[:, 8:].reshape(PLEN, 256).astype(BF)
    for j in range(NY):
        both = jnp.concatenate([pl_buf[j, 0, :, 256:], pl_buf[j, 1, :, 256:]], axis=1)
        rotary[j * 16 : (j + 1) * 16, :] = both
        rotary[64 + j * 16 : 64 + (j + 1) * 16, :] = both

    for pair in range(2):
        outs = []
        for sub in range(2):
            i = pair * 2 + sub
            prompt_scores = dot_nt(absorbed[i], latent[...]) + jnp.dot(
                own_turned(i), rotary[...], preferred_element_type=F32
            )
            own_scores = own_buf[i]
            top = jnp.max(
                jnp.maximum(jnp.maximum(prompt_scores[:, :128], prompt_scores[:, 128:]), own_scores),
                axis=1,
                keepdims=True,
            )
            prompt_exp = jnp.exp2((prompt_scores - top) * (SCALE * LOG2E))
            own_exp = jnp.exp2((own_scores - top) * (SCALE * LOG2E))
            total = jnp.sum(prompt_exp[:, :128] + prompt_exp[:, 128:] + own_exp, axis=1, keepdims=True)
            factor = jnp.where(live, 1.0 / total, 0.0)
            own_weight = own_exp.astype(BF)
            mixed = jnp.dot(prompt_exp.astype(BF), latent[...], preferred_element_type=F32)
            mixed_own = jnp.concatenate(
                [
                    jnp.dot(own_weight[:128], fresh[:128, :], preferred_element_type=F32),
                    jnp.dot(own_weight[128:], fresh[128:, :], preferred_element_type=F32),
                ],
                axis=0,
            )
            mixed = ((mixed + mixed_own) * factor).astype(BF)
            out = jnp.dot(mixed, vu[:, i * 128 : (i + 1) * 128], preferred_element_type=F32)
            outs.append(out.reshape(32, 8, 128))
        o_send[pair] = jnp.concatenate(outs, axis=1).astype(BF)

        @pl.loop(1, 32)
        def _(d):
            there = lax.rem(h + d, 32)
            remote(o_send.at[pair, there], out_ref.at[pair, h], o_ssem.at[pair], o_rsem.at[pair], (g, there)).start()

        keep = pltpu.make_async_copy(o_send.at[pair, h], out_ref.at[pair, h], local_sem.at[5 + pair])
        keep.start()

    for copy in w_out + wf_out + wc_out + k_out + q_out + qy_out + kz_out + p_out + pz_out + pg_out + py_out:
        copy.wait_send()
    for pair in range(2):
        pltpu.make_async_copy(o_send.at[pair, h], out_ref.at[pair, h], local_sem.at[5 + pair]).wait()
        whole = remote(
            o_send.at[pair, pl.ds(0, 31)], out_ref.at[pair, pl.ds(0, 31)], o_ssem.at[pair], o_rsem.at[pair], sibling
        )
        whole.wait_send()
        whole.wait_recv()


def local(
    query_latent, response_keys, prompt_cache, owners, lengths, w_query_plain, w_query_rotary, w_key_up, w_value_up
):
    vmem = pl.BlockSpec(memory_space=pltpu.VMEM)
    hbm = pl.BlockSpec(memory_space=pl.ANY)
    dma = pltpu.SemaphoreType.DMA
    gathered = pl.pallas_call(
        kernel,
        out_shape=jax.ShapeDtypeStruct((2, 32, 16, 128), BF),
        in_specs=[hbm] * 10,
        out_specs=vmem,
        scratch_shapes=[
            pltpu.SMEM((1,), jnp.int32),
            pltpu.VMEM((8, QLAT), BF),
            pltpu.VMEM((8, 576), BF),
            pltpu.VMEM((1, 16), jnp.int32),
            pltpu.VMEM((32, 256), F32),
            pltpu.VMEM((QLAT, 768), BF),
            pltpu.VMEM((512, 512), BF),
            pltpu.VMEM((512, 512), BF),
            pltpu.VMEM((1, 147456), BF),
            pltpu.VMEM((PLEN, 512), F32),
            pltpu.VMEM((16, 768), BF),
            pltpu.VMEM((16, 256), BF),
            pltpu.VMEM((16, 128), BF),
            pltpu.VMEM((32, 16, 768), BF),
            pltpu.VMEM((NY, NZ, 16, 256), BF),
            pltpu.VMEM((NY, 16, 128), BF),
            pltpu.VMEM((NZ, 16, 128), BF),
            pltpu.VMEM((NY, NZ, 16, 256), BF),
            pltpu.VMEM((NY, 2, 16, 128), BF),
            pltpu.VMEM((NY, NZ, 16, 256), BF),
            pltpu.VMEM((NY, 2, 16, 128), BF),
            pltpu.VMEM((NZ, 16, 384), BF),
            pltpu.VMEM((NZ, 16, 384), BF),
            pltpu.VMEM((NY, NZ, 16, 384), BF),
            pltpu.VMEM((TOK, QLAT), BF),
            pltpu.VMEM((TOK, 512), BF),
            pltpu.VMEM((TOK, 128), BF),
            pltpu.VMEM((PLEN, 512), BF),
            pltpu.VMEM((128, PLEN), BF),
            pltpu.VMEM((TOK, 512), BF),
            pltpu.VMEM((TOK, 256), BF),
            pltpu.VMEM((4, TOK, 512), BF),
            pltpu.VMEM((4, TOK, 128), F32),
            pltpu.VMEM((2, 32, 16, 128), BF),
            dma((12,)),
            *[dma((4, 2))] * 2,
            *[dma((2,))] * 2,
            *[dma((4, 2))] * 2,
            *[dma((8,))] * 2,
            *[dma((4,))] * 2,
            *[dma((4, 2))] * 2,
            *[dma((8, 2))] * 2,
            *[dma((4, 2))] * 2,
            *[dma((8,))] * 4,
            *[dma((4, 2))] * 2,
            *[dma((2,))] * 2,
        ],
        compiler_params=pltpu.CompilerParams(collective_id=0, has_side_effects=True, vmem_limit_bytes=60 << 20),
    )(
        owners,
        query_latent,
        response_keys,
        lengths,
        jnp.asarray(rotary_tables()),
        prompt_cache,
        w_query_plain,
        w_query_rotary,
        w_key_up,
        w_value_up,
    )
    return gathered.reshape(2, 32, 2, 8, 128).transpose(3, 1, 0, 2, 4).reshape(8, 16384)


def solution(mesh):
    return jax.shard_map(
        local,
        mesh=mesh,
        in_specs=(
            P(("group", "head"), None),
            P(("group", "head"), None),
            P(("group", "head"), None),
            P("group"),
            P("group", None),
            P("group", "head"),
            P("group", "head"),
            P("head", None),
            P(None, "head"),
        ),
        out_specs=P(("group", "head"), None),
        check_vma=False,
    )
```

```python
import math

import jax
import jax.numpy as jnp
import numpy as np
from jax import lax
from jax.experimental import pallas as pl
from jax.experimental.pallas import tpu as pltpu
from jax.sharding import PartitionSpec as P

MESH = pl.DeviceIdType.MESH
LAT = 512
ROPE = 64
NOPE = 128
VDIM = 128
QLAT = 1536
PLEN = 256
RTOK = 16
TOK = 256
NX, NY, NZ = 4, 4, 8
SHARD = 192
HALF = 96
BF = jnp.bfloat16
F32 = jnp.float32
SCALE = 1.0 / math.sqrt(NOPE + ROPE)
LOG2E = 1.4426950408889634


def rotary_tables():
    position = (PLEN + np.arange(RTOK)).astype(np.float32)
    inverse = np.exp(np.arange(32).astype(np.float32) * np.float32(-2.0 * math.log(10000.0) / ROPE))
    angle = (position[:, None] * inverse[None, :].astype(np.float32)).astype(np.float32)
    cosine, sine = np.cos(angle), np.sin(angle)
    cos_table = np.tile(np.concatenate([cosine, cosine], 1), (1, 4))
    sin_table = np.tile(np.concatenate([-sine, sine], 1), (1, 4))
    return np.concatenate([cos_table, sin_table], 0).astype(np.float32)


def dot_nt(a, b):
    return lax.dot_general(a, b, (((1,), (1,)), ((), ())), preferred_element_type=F32)


def kernel(
    owner_hbm, query_hbm, keys_hbm, length_hbm, table_hbm, prompt_hbm, wp_hbm, wr_hbm, ku_hbm, vu_hbm,
    out_ref,
    owner_ref, query_ref, keys_ref, length_ref, table_ref, w, ku, vu, flat, stage, q_send, k_send, r_own, qb, kl, kt, kr,
    p_send, r_send, p_recv, r_recv, z_send, z_recv, pl_buf,
    x_buf, fresh, fresh_rot, latent, rotary, plain, turned, absorbed, own_buf, o_send,
    local_sem, wx_send, wx_recv, wf_send, wf_recv, wc_send, wc_recv,
    qz_send, qz_recv, qy_send, qy_recv, qf_send, qf_recv, ky_send, ky_recv, kz_send, kz_recv,
    pa_send, pa_recv, pz_send, pz_recv, pg_send, pg_recv, py_send, py_recv,
    o_ssem, o_rsem,
):
    g = lax.axis_index("group")
    h = lax.axis_index("head")
    x, c = g // 2, g % 2
    y, z = h // NZ, h % NZ

    def at_x(d):
        return (lax.rem(x + d, NX) * 2 + c, h)

    def at_y(d):
        return (g, lax.rem(y + d, NY) * NZ + z)

    def at_z(d):
        return (g, y * NZ + lax.rem(z + d, NZ))

    sibling = (x * 2 + 1 - c, h)
    y_order = (1, 3, 2)
    z_order = (4, 3, 5, 2, 6, 1, 7)

    def remote(src, dst, ssem, rsem, device):
        return pltpu.make_async_remote_copy(src, dst, ssem, rsem, device_id=device, device_id_type=MESH)

    barrier = pltpu.get_barrier_semaphore()
    peers = [sibling] + [at_x(d) for d in (1, 3)] + [at_y(d) for d in y_order] + [at_z(d) for d in z_order]
    for peer in peers:
        pl.semaphore_signal(barrier, inc=1, device_id=peer, device_id_type=MESH)

    def half_rows(dx, core, half):
        start = (lax.rem(x + dx + NX, NX) * 2 + core) * SHARD + half * HALF
        return pl.ds(pl.multiple_of(start, 32), HALF)

    mine = pl.ds(pl.multiple_of(g * SHARD, 64), SHARD)
    flat_copy = pltpu.make_async_copy(prompt_hbm, flat, local_sem.at[0])
    query_copy = pltpu.make_async_copy(query_hbm, query_ref, local_sem.at[7])
    keys_copy = pltpu.make_async_copy(keys_hbm, keys_ref, local_sem.at[8])
    wp_copy = pltpu.make_async_copy(wp_hbm, w.at[mine, 0:512], local_sem.at[3])
    wr_copy = pltpu.make_async_copy(wr_hbm, w.at[mine, 512:768], local_sem.at[4])
    owner_copy = pltpu.make_async_copy(owner_hbm, owner_ref, local_sem.at[9])
    length_copy = pltpu.make_async_copy(length_hbm, length_ref, local_sem.at[10])
    table_copy = pltpu.make_async_copy(table_hbm, table_ref, local_sem.at[11])
    ku_copy = pltpu.make_async_copy(ku_hbm, ku, local_sem.at[1])
    vu_copy = pltpu.make_async_copy(vu_hbm, vu, local_sem.at[2])
    for copy in (
        flat_copy, query_copy, keys_copy, wp_copy, wr_copy, owner_copy, length_copy, table_copy, ku_copy, vu_copy
    ):
        copy.start()

    flat_copy.wait()

    @pl.loop(0, PLEN // 8)
    def _(block):
        for r in range(8):
            row = flat[0:1, pl.ds(pl.multiple_of(block * 4096 + r * 512, 512), 512)].astype(F32)
            stage[pl.ds(block * 8 + r, 1), :] = row
        both = stage[pl.ds(pl.multiple_of(block * 8, 8), 8), :]
        p_send[pl.ds(block // 8, 1), pl.ds(block % 8, 1)] = jnp.concatenate(
            [both[:, :256], both[:, 256:]], axis=0
        ).astype(BF)[None, None]

    @pl.loop(0, NY)
    def _(j):
        for r in range(16):
            row = flat[0:1, pl.ds(pl.multiple_of(PLEN * LAT + j * 4096 + r * 256, 256), 256)].astype(F32)
            stage[pl.ds(r, 1), 0:256] = row
        both = stage[0:16, 0:256].astype(BF)
        r_send[pl.ds(j, 1), 0:1] = both[None, None, :, :128]
        r_send[pl.ds(j, 1), 1:2] = both[None, None, :, 128:]

    p_recv[pl.ds(y, 1)] = p_send[pl.ds(y, 1)]
    r_recv[pl.ds(y, 1)] = r_send[pl.ds(y, 1)]

    query_copy.wait()
    query = query_ref[...].astype(F32)
    packed = jnp.concatenate([query[:, :768], query[:, 768:]], axis=0).astype(BF)
    q_send[...] = packed
    qb[pl.ds(h, 1)] = packed[None]
    keys_copy.wait()
    keys = keys_ref[...].astype(F32)
    packed = jnp.concatenate([keys[:, :256], keys[:, 256:512]], axis=0).astype(BF)
    k_send[...] = packed
    kl[pl.ds(y, 1), pl.ds(z, 1)] = packed[None, None]
    rot = jnp.concatenate([keys[:, 512:], keys[:, 512:]], axis=1)
    packed = jnp.concatenate([rot, rot], axis=0).astype(BF)
    r_own[...] = packed
    kt[pl.ds(y, 1)] = packed[None]
    wp_copy.wait()
    wr_copy.wait()

    pl.semaphore_wait(barrier, len(peers))

    p_out, k_out = [], []
    for d in y_order:
        there = lax.rem(y + d, NY)
        k_out.append(remote(k_send, kl.at[y, z], ky_send.at[d, 0], ky_recv.at[d, 0], at_y(d)))
        k_out.append(remote(r_own, kt.at[y], ky_send.at[d, 1], ky_recv.at[d, 1], at_y(d)))
        p_out.append(remote(p_send.at[there], p_recv.at[y], pa_send.at[d, 0], pa_recv.at[d, 0], at_y(d)))
        p_out.append(remote(r_send.at[there], r_recv.at[y], pa_send.at[d, 1], pa_recv.at[d, 1], at_y(d)))
    q_out = [remote(q_send, qb.at[h], qz_send.at[d], qz_recv.at[d], at_z(d)) for d in z_order]
    w_out = []
    for step in range(2):
        for d in (1, 3):
            half = step if d == 1 else 1 - step
            rows = w.at[half_rows(0, c, half)]
            w_out.append(remote(rows, rows, wx_send.at[d, half], wx_recv.at[d, half], at_x(d)))
    for copy in p_out + k_out + q_out + w_out:
        copy.start()
    wc_out = []

    def to_sibling(dx, half):
        rows = w.at[half_rows(dx, c, half)]
        wc_out.append(remote(rows, rows, wc_send.at[dx, half], wc_recv.at[dx, half], sibling))
        wc_out[-1].start()

    def from_sibling(dx, half):
        rows = w.at[half_rows(dx, 1 - c, half)]
        remote(rows, rows, wc_send.at[dx, half], wc_recv.at[dx, half], sibling).wait_recv()

    def arrived(d, half):
        rows = w.at[half_rows(NX - d, c, half)]
        remote(rows, rows, wx_send.at[d, half], wx_recv.at[d, half], at_x(d)).wait_recv()

    to_sibling(0, 0)
    to_sibling(0, 1)

    for copy in k_out:
        copy.wait_recv()
    tiles = kt[...].astype(F32)
    tile_row = lax.broadcasted_iota(jnp.int32, (16, 128), 0)
    tile_lane = lax.broadcasted_iota(jnp.int32, (16, 128), 1)
    upper = jnp.where(tile_lane < 64, tiles[0], tiles[1])
    lower = jnp.where(tile_lane < 64, tiles[2], tiles[3])
    kr[pl.ds(z, 1)] = jnp.where(tile_row < 8, upper, lower).astype(BF)[None]
    kz_out, kf_out = [], []

    def at(d):
        return lax.rem(z + d + NZ, NZ)

    def key_hop(copies, n, d, source, rows):
        part = kl.at[rows, at(source)]
        copies.append(remote(part, part, kz_send.at[n, 0], kz_recv.at[n, 0], at_z(d)))
        if n != 7:
            part = kr.at[at(source)]
            copies.append(remote(part, part, kz_send.at[n, 1], kz_recv.at[n, 1], at_z(d)))

    every = slice(0, NY)
    for n, d in enumerate((2, 6, 1, 7)):
        key_hop(kz_out, n, d, 0, every)
    key_hop(kf_out, 4, 6, 2, slice(0, 2))
    key_hop(kf_out, 7, 2, -2, slice(2, 4))
    key_hop(kf_out, 5, 1, -2, every)
    key_hop(kf_out, 6, 7, 2, every)

    wf_out = []

    def pass_on(d, half):
        arrived(d, half)
        rows = w.at[half_rows(NX - d, c, half)]
        wf_out.append(remote(rows, rows, wf_send.at[half], wf_recv.at[half], at_x(d)))
        wf_out[-1].start()
        to_sibling(NX - d, half)

    owner_copy.wait()
    owner = owner_ref[0, 0]
    for copy in p_out:
        copy.wait_recv()
    chosen = p_recv[owner // NZ]
    chosen_rot = r_recv[owner // NZ]
    for k in range(NZ):
        z_send[k] = jnp.concatenate([chosen[k], chosen_rot[k % 2]], axis=1)
    pz_out = []
    for d in z_order:
        pz_out.append(remote(z_send.at[lax.rem(z + d, NZ)], z_recv.at[z], pz_send.at[d], pz_recv.at[d], at_z(d)))
    for copy in pz_out:
        copy.start()
    z_recv[pl.ds(z, 1)] = z_send[pl.ds(z, 1)]

    pass_on(1, 0)
    pass_on(3, 1)

    for copy in q_out:
        copy.wait_recv()

    def query_rows(dy, half):
        return qb.at[pl.ds(lax.rem(y + dy + NY, NY) * NZ + half * 4, 4)]

    qy_out, qf_out = [], []
    for step in range(2):
        for d in (1, 3):
            half = step if d == 1 else 1 - step
            part = query_rows(0, half)
            qy_out.append(remote(part, part, qy_send.at[d, half], qy_recv.at[d, half], at_y(d)))
    for copy in qy_out + kz_out:
        copy.start()

    for copy in pz_out:
        copy.wait_recv()
    pl_buf[pl.ds(y, 1), pl.ds(z, 1)] = z_recv[owner % NZ][None, None]
    pg_out = [remote(pl_buf.at[y, z], pl_buf.at[y, z], pg_send.at[d], pg_recv.at[d], at_z(d)) for d in z_order]
    for copy in pg_out:
        copy.start()
    for copy in kz_out:
        copy.wait_recv()
    for copy in kf_out:
        copy.start()
    for n, (d, half) in enumerate(((1, 0), (3, 1))):
        qy_out[n].wait_recv()
        part = query_rows(-1 if d == 1 else 1, half)
        qf_out.append(remote(part, part, qf_send.at[half], qf_recv.at[half], at_y(d)))
        qf_out[-1].start()

    arrived(1, 1)
    to_sibling(3, 1)
    arrived(3, 0)
    to_sibling(1, 0)
    for half in range(2):
        rows = w.at[half_rows(2, c, half)]
        remote(rows, rows, wf_send.at[half], wf_recv.at[half], sibling).wait_recv()
        to_sibling(2, half)

    for copy in pg_out:
        copy.wait_recv()
    py_out = []
    for d in y_order:
        part = pl_buf.at[y, :, :, 0:256]
        py_out.append(remote(part, part, py_send.at[d, 0], py_recv.at[d, 0], at_y(d)))
        part = pl_buf.at[y, 0:2, :, 256:384]
        py_out.append(remote(part, part, py_send.at[d, 1], py_recv.at[d, 1], at_y(d)))
    for copy in py_out:
        copy.start()

    for copy in qy_out[2:] + qf_out:
        copy.wait_recv()
    gathered = qb[...].astype(F32)
    x_buf[:, :768] = gathered[:, :8].reshape(TOK, 768).astype(BF)
    x_buf[:, 768:] = gathered[:, 8:].reshape(TOK, 768).astype(BF)
    for dx in range(NX):
        for half in range(2):
            from_sibling(dx, half)
    both = jnp.dot(x_buf[...], w[...], preferred_element_type=F32)
    plain[...] = both[:, :512].astype(BF)
    spun = both[:, 512:]
    lane = lax.broadcasted_iota(jnp.int32, (TOK, 256), 1)
    swapped = jnp.where(lane % 64 < 32, pltpu.roll(spun, 224, 1), pltpu.roll(spun, 32, 1))
    table_copy.wait()
    cosine = jnp.broadcast_to(table_ref[:16][None], (16, 16, 256)).reshape(TOK, 256)
    sine = jnp.broadcast_to(table_ref[16:][None], (16, 16, 256)).reshape(TOK, 256)
    turned[...] = (spun * cosine + swapped * sine).astype(BF)

    ku_copy.wait()
    for i in range(4):
        absorbed[i] = jnp.dot(
            plain[:, i * 128 : (i + 1) * 128], ku[i * 128 : (i + 1) * 128, :], preferred_element_type=F32
        ).astype(BF)

    for copy in kf_out:
        copy.wait_recv()
    gathered = kl[...].astype(F32).reshape(32, 16, 256)
    fresh[:, :256] = gathered[:, :8].reshape(TOK, 256).astype(BF)
    fresh[:, 256:] = gathered[:, 8:].reshape(TOK, 256).astype(BF)
    gathered = kr[...].astype(F32)
    rot_lane = lax.broadcasted_iota(jnp.int32, (64, 128), 1)
    for j in range(NY):
        piece = gathered[:, (j // 2) * 8 : (j // 2) * 8 + 8].reshape(64, 128)
        piece = jnp.where((rot_lane < 64) if j % 2 == 0 else (rot_lane >= 64), piece, 0.0)
        fresh_rot[j * 64 : (j + 1) * 64, :] = (piece + pltpu.roll(piece, 64, 1)).astype(BF)

    length_copy.wait()
    lengths = jnp.broadcast_to(length_ref[...], (TOK, 16))
    token = lax.broadcasted_iota(jnp.int32, (TOK, 16), 0)
    slot = lax.broadcasted_iota(jnp.int32, (TOK, 16), 1)
    limit = jnp.sum(jnp.where(token // RTOK == slot, lengths, 0).astype(F32), axis=1, keepdims=True)
    place = (lax.broadcasted_iota(jnp.int32, (TOK, 1), 0) % RTOK).astype(F32)
    live = place < limit

    t_half = lax.broadcasted_iota(jnp.int32, (128, 128), 0)
    s_half = lax.broadcasted_iota(jnp.int32, (128, 128), 1)
    allowed = (t_half // RTOK == s_half // RTOK) & (s_half <= t_half)
    pair_lane = lax.broadcasted_iota(jnp.int32, (TOK, 128), 1)

    def own_turned(i):
        mine_lanes = (pair_lane < 64) if i % 2 == 0 else (pair_lane >= 64)
        part = turned[:, (i // 2) * 128 : (i // 2 + 1) * 128].astype(F32)
        return jnp.where(mine_lanes, part, 0.0).astype(BF)

    for i in range(4):
        t = own_turned(i)
        for half in range(2):
            part = slice(half * 128, (half + 1) * 128)
            scores = dot_nt(absorbed[i, part, :], fresh[part, :]) + dot_nt(t[part], fresh_rot[part, :])
            own_buf[i, part, :] = jnp.where(allowed, scores, -jnp.inf)
    vu_copy.wait()

    for copy in py_out:
        copy.wait_recv()
    gathered = pl_buf[:, :, :, :256].astype(F32).reshape(32, 16, 256)
    latent[:, :256] = gathered[:, :8].reshape(PLEN, 256).astype(BF)
    latent[:, 256:] = gathered[:, 8:].reshape(PLEN, 256).astype(BF)
    for j in range(NY):
        both = jnp.concatenate([pl_buf[j, 0, :, 256:], pl_buf[j, 1, :, 256:]], axis=1)
        rotary[j * 16 : (j + 1) * 16, :] = both
        rotary[64 + j * 16 : 64 + (j + 1) * 16, :] = both

    for pair in range(2):
        outs = []
        for sub in range(2):
            i = pair * 2 + sub
            prompt_scores = dot_nt(absorbed[i], latent[...]) + jnp.dot(
                own_turned(i), rotary[...], preferred_element_type=F32
            )
            own_scores = own_buf[i]
            top = jnp.max(
                jnp.maximum(jnp.maximum(prompt_scores[:, :128], prompt_scores[:, 128:]), own_scores),
                axis=1,
                keepdims=True,
            )
            prompt_exp = jnp.exp2((prompt_scores - top) * (SCALE * LOG2E))
            own_exp = jnp.exp2((own_scores - top) * (SCALE * LOG2E))
            total = jnp.sum(prompt_exp[:, :128] + prompt_exp[:, 128:] + own_exp, axis=1, keepdims=True)
            factor = jnp.where(live, 1.0 / total, 0.0)
            own_weight = own_exp.astype(BF)
            mixed = jnp.dot(prompt_exp.astype(BF), latent[...], preferred_element_type=F32)
            mixed_own = jnp.concatenate(
                [
                    jnp.dot(own_weight[:128], fresh[:128, :], preferred_element_type=F32),
                    jnp.dot(own_weight[128:], fresh[128:, :], preferred_element_type=F32),
                ],
                axis=0,
            )
            mixed = ((mixed + mixed_own) * factor).astype(BF)
            out = jnp.dot(mixed, vu[:, i * 128 : (i + 1) * 128], preferred_element_type=F32)
            outs.append(out.reshape(32, 8, 128))
        o_send[pair] = jnp.concatenate(outs, axis=1).astype(BF)

        @pl.loop(1, 32)
        def _(d):
            there = lax.rem(h + d, 32)
            remote(o_send.at[pair, there], out_ref.at[h, pair], o_ssem.at[pair], o_rsem.at[pair], (g, there)).start()

        keep = pltpu.make_async_copy(o_send.at[pair, h], out_ref.at[h, pair], local_sem.at[5 + pair])
        keep.start()

    for copy in w_out + wf_out + wc_out + k_out + q_out + qy_out + qf_out + kz_out + kf_out + p_out + pz_out + pg_out + py_out:
        copy.wait_send()
    for pair in range(2):
        pltpu.make_async_copy(o_send.at[pair, h], out_ref.at[h, pair], local_sem.at[5 + pair]).wait()
        whole = remote(
            o_send.at[pair, pl.ds(0, 31)], out_ref.at[pl.ds(0, 31), pair], o_ssem.at[pair], o_rsem.at[pair], sibling
        )
        whole.wait_send()
        whole.wait_recv()


def local(
    query_latent, response_keys, prompt_cache, owners, lengths, w_query_plain, w_query_rotary, w_key_up, w_value_up
):
    vmem = pl.BlockSpec(memory_space=pltpu.VMEM)
    hbm = pl.BlockSpec(memory_space=pltpu.HBM)
    dma = pltpu.SemaphoreType.DMA
    gathered = pl.pallas_call(
        kernel,
        out_shape=jax.ShapeDtypeStruct((32, 2, 16, 128), BF),
        in_specs=[hbm] * 10,
        out_specs=hbm,
        scratch_shapes=[
            pltpu.SMEM((1, 1), jnp.int32),
            pltpu.VMEM((8, QLAT), BF),
            pltpu.VMEM((8, 576), BF),
            pltpu.VMEM((1, 16), jnp.int32),
            pltpu.VMEM((32, 256), F32),
            pltpu.VMEM((QLAT, 768), BF),
            pltpu.VMEM((512, 512), BF),
            pltpu.VMEM((512, 512), BF),
            pltpu.VMEM((1, 147456), BF),
            pltpu.VMEM((PLEN, 512), F32),
            pltpu.VMEM((16, 768), BF),
            pltpu.VMEM((16, 256), BF),
            pltpu.VMEM((16, 128), BF),
            pltpu.VMEM((32, 16, 768), BF),
            pltpu.VMEM((NY, NZ, 16, 256), BF),
            pltpu.VMEM((NY, 16, 128), BF),
            pltpu.VMEM((NZ, 16, 128), BF),
            pltpu.VMEM((NY, NZ, 16, 256), BF),
            pltpu.VMEM((NY, 2, 16, 128), BF),
            pltpu.VMEM((NY, NZ, 16, 256), BF),
            pltpu.VMEM((NY, 2, 16, 128), BF),
            pltpu.VMEM((NZ, 16, 384), BF),
            pltpu.VMEM((NZ, 16, 384), BF),
            pltpu.VMEM((NY, NZ, 16, 384), BF),
            pltpu.VMEM((TOK, QLAT), BF),
            pltpu.VMEM((TOK, 512), BF),
            pltpu.VMEM((TOK, 128), BF),
            pltpu.VMEM((PLEN, 512), BF),
            pltpu.VMEM((128, PLEN), BF),
            pltpu.VMEM((TOK, 512), BF),
            pltpu.VMEM((TOK, 256), BF),
            pltpu.VMEM((4, TOK, 512), BF),
            pltpu.VMEM((4, TOK, 128), F32),
            pltpu.VMEM((2, 32, 16, 128), BF),
            dma((12,)),
            *[dma((4, 2))] * 2,
            *[dma((2,))] * 2,
            *[dma((4, 2))] * 2,
            *[dma((8,))] * 2,
            *[dma((4, 2))] * 2,
            *[dma((2,))] * 2,
            *[dma((4, 2))] * 2,
            *[dma((8, 2))] * 2,
            *[dma((4, 2))] * 2,
            *[dma((8,))] * 4,
            *[dma((4, 2))] * 2,
            *[dma((2,))] * 2,
        ],
        compiler_params=pltpu.CompilerParams(collective_id=0, has_side_effects=True, vmem_limit_bytes=60 << 20),
    )(
        owners.reshape(1, 1),
        query_latent,
        response_keys,
        lengths,
        jnp.asarray(rotary_tables()),
        prompt_cache,
        w_query_plain,
        w_query_rotary,
        w_key_up,
        w_value_up,
    )
    return gathered.reshape(32, 2, 2, 8, 128).transpose(3, 0, 1, 2, 4).reshape(8, 16384)


def solution(mesh):
    return jax.shard_map(
        local,
        mesh=mesh,
        in_specs=(
            P(("group", "head"), None),
            P(("group", "head"), None),
            P(("group", "head"), None),
            P("group"),
            P("group", None),
            P("group", "head"),
            P("group", "head"),
            P("head", None),
            P(None, "head"),
        ),
        out_specs=P(("group", "head"), None),
        check_vma=False,
    )
```

```python
import math

import jax
import jax.numpy as jnp
import numpy as np
from jax import lax
from jax.experimental import pallas as pl
from jax.experimental.pallas import tpu as pltpu
from jax.sharding import PartitionSpec as P

MESH = pl.DeviceIdType.MESH
LAT = 512
ROPE = 64
NOPE = 128
VDIM = 128
QLAT = 1536
PLEN = 256
RTOK = 16
TOK = 256
NX, NY, NZ = 4, 4, 8
SHARD = 192
HALF = 96
BF = jnp.bfloat16
F32 = jnp.float32
SCALE = 1.0 / math.sqrt(NOPE + ROPE)
LOG2E = 1.4426950408889634


def rotary_tables():
    position = (PLEN + np.arange(RTOK)).astype(np.float32)
    inverse = np.exp(np.arange(32).astype(np.float32) * np.float32(-2.0 * math.log(10000.0) / ROPE))
    angle = (position[:, None] * inverse[None, :].astype(np.float32)).astype(np.float32)
    cosine, sine = np.cos(angle), np.sin(angle)
    cos_table = np.tile(np.concatenate([cosine, cosine], 1), (1, 4))
    sin_table = np.tile(np.concatenate([-sine, sine], 1), (1, 4))
    return np.concatenate([cos_table, sin_table], 0).astype(np.float32)


def dot_nt(a, b):
    return lax.dot_general(a, b, (((1,), (1,)), ((), ())), preferred_element_type=F32)


def kernel(
    owner_hbm, query_hbm, keys_hbm, length_hbm, table_hbm, prompt_hbm, wp_hbm, wr_hbm, ku_hbm, vu_hbm,
    out_ref,
    owner_ref, query_ref, keys_ref, length_ref, table_ref, w, ku, vu, flat, stage, q_send, k_send, r_own, qb, kl, kt, kr,
    p_send, r_send, p_recv, r_recv, z_send, z_recv, pl_buf,
    x_buf, fresh, fresh_rot, latent, rotary, plain, turned, absorbed, own_buf, o_send,
    local_sem, wx_send, wx_recv, wf_send, wf_recv, wc_send, wc_recv,
    qz_send, qz_recv, qy_send, qy_recv, qf_send, qf_recv, ky_send, ky_recv, kz_send, kz_recv,
    pa_send, pa_recv, pz_send, pz_recv, pg_send, pg_recv, py_send, py_recv,
    o_ssem, o_rsem, ready,
):
    g = lax.axis_index("group")
    h = lax.axis_index("head")
    x, c = g // 2, g % 2
    y, z = h // NZ, h % NZ

    def at_x(d):
        return (lax.rem(x + d, NX) * 2 + c, h)

    def at_y(d):
        return (g, lax.rem(y + d, NY) * NZ + z)

    def at_z(d):
        return (g, y * NZ + lax.rem(z + d, NZ))

    sibling = (x * 2 + 1 - c, h)
    y_order = (1, 3, 2)
    z_far, z_near = (4, 3, 5), (2, 6, 1, 7)
    z_order = z_far + z_near

    def remote(src, dst, ssem, rsem, device):
        return pltpu.make_async_remote_copy(src, dst, ssem, rsem, device_id=device, device_id_type=MESH)

    barrier = pltpu.get_barrier_semaphore()
    peers = [sibling] + [at_x(d) for d in (1, 3)] + [at_y(d) for d in y_order] + [at_z(d) for d in z_near]
    for peer in peers:
        pl.semaphore_signal(barrier, inc=1, device_id=peer, device_id_type=MESH)

    def half_rows(dx, core, half):
        start = (lax.rem(x + dx + NX, NX) * 2 + core) * SHARD + half * HALF
        return pl.ds(pl.multiple_of(start, 32), HALF)

    mine = pl.ds(pl.multiple_of(g * SHARD, 64), SHARD)
    flat_copy = pltpu.make_async_copy(prompt_hbm, flat, local_sem.at[0])
    query_copy = pltpu.make_async_copy(query_hbm, query_ref, local_sem.at[7])
    keys_copy = pltpu.make_async_copy(keys_hbm, keys_ref, local_sem.at[8])
    wp_copy = pltpu.make_async_copy(wp_hbm, w.at[mine, 0:512], local_sem.at[3])
    wr_copy = pltpu.make_async_copy(wr_hbm, w.at[mine, 512:768], local_sem.at[4])
    owner_copy = pltpu.make_async_copy(owner_hbm, owner_ref, local_sem.at[9])
    length_copy = pltpu.make_async_copy(length_hbm, length_ref, local_sem.at[10])
    table_copy = pltpu.make_async_copy(table_hbm, table_ref, local_sem.at[11])
    ku_copy = pltpu.make_async_copy(ku_hbm, ku, local_sem.at[1])
    vu_copy = pltpu.make_async_copy(vu_hbm, vu, local_sem.at[2])
    for copy in (
        flat_copy, query_copy, keys_copy, wp_copy, wr_copy, owner_copy, length_copy, table_copy, ku_copy, vu_copy
    ):
        copy.start()

    flat_copy.wait()

    @pl.loop(0, PLEN // 8)
    def _(block):
        for r in range(8):
            row = flat[0:1, pl.ds(pl.multiple_of(block * 4096 + r * 512, 512), 512)].astype(F32)
            stage[pl.ds(block * 8 + r, 1), :] = row
        both = stage[pl.ds(pl.multiple_of(block * 8, 8), 8), :]
        p_send[pl.ds(block // 8, 1), pl.ds(block % 8, 1)] = jnp.concatenate(
            [both[:, :256], both[:, 256:]], axis=0
        ).astype(BF)[None, None]

    @pl.loop(0, NY)
    def _(j):
        for r in range(16):
            row = flat[0:1, pl.ds(pl.multiple_of(PLEN * LAT + j * 4096 + r * 256, 256), 256)].astype(F32)
            stage[pl.ds(r, 1), 0:256] = row
        both = stage[0:16, 0:256].astype(BF)
        r_send[pl.ds(j, 1), 0:1] = both[None, None, :, :128]
        r_send[pl.ds(j, 1), 1:2] = both[None, None, :, 128:]

    p_recv[pl.ds(y, 1)] = p_send[pl.ds(y, 1)]
    r_recv[pl.ds(y, 1)] = r_send[pl.ds(y, 1)]

    query_copy.wait()
    query = query_ref[...].astype(F32)
    packed = jnp.concatenate([query[:, :768], query[:, 768:]], axis=0).astype(BF)
    q_send[...] = packed
    qb[pl.ds(h, 1)] = packed[None]
    keys_copy.wait()
    keys = keys_ref[...].astype(F32)
    packed = jnp.concatenate([keys[:, :256], keys[:, 256:512]], axis=0).astype(BF)
    k_send[...] = packed
    kl[pl.ds(y, 1), pl.ds(z, 1)] = packed[None, None]
    rot = jnp.concatenate([keys[:, 512:], keys[:, 512:]], axis=1)
    packed = jnp.concatenate([rot, rot], axis=0).astype(BF)
    r_own[...] = packed
    kt[pl.ds(y, 1)] = packed[None]
    wp_copy.wait()
    wr_copy.wait()

    pl.semaphore_wait(barrier, len(peers))
    for d in (2, 6):
        pl.semaphore_signal(ready, inc=1, device_id=at_z(d), device_id_type=MESH)

    p_out, k_out = [], []
    for d in y_order:
        there = lax.rem(y + d, NY)
        k_out.append(remote(k_send, kl.at[y, z], ky_send.at[d, 0], ky_recv.at[d, 0], at_y(d)))
        k_out.append(remote(r_own, kt.at[y], ky_send.at[d, 1], ky_recv.at[d, 1], at_y(d)))
        p_out.append(remote(p_send.at[there], p_recv.at[y], pa_send.at[d, 0], pa_recv.at[d, 0], at_y(d)))
        p_out.append(remote(r_send.at[there], r_recv.at[y], pa_send.at[d, 1], pa_recv.at[d, 1], at_y(d)))
    q_out = [remote(q_send, qb.at[h], qz_send.at[d], qz_recv.at[d], at_z(d)) for d in z_near + z_far]
    w_out = []
    for step in range(2):
        for d in (1, 3):
            half = step if d == 1 else 1 - step
            rows = w.at[half_rows(0, c, half)]
            w_out.append(remote(rows, rows, wx_send.at[d, half], wx_recv.at[d, half], at_x(d)))
    for copy in p_out + k_out + q_out[:4] + w_out:
        copy.start()
    wc_out = []

    def to_sibling(dx, half):
        rows = w.at[half_rows(dx, c, half)]
        wc_out.append(remote(rows, rows, wc_send.at[dx, half], wc_recv.at[dx, half], sibling))
        wc_out[-1].start()

    def from_sibling(dx, half):
        rows = w.at[half_rows(dx, 1 - c, half)]
        remote(rows, rows, wc_send.at[dx, half], wc_recv.at[dx, half], sibling).wait_recv()

    def arrived(d, half):
        rows = w.at[half_rows(NX - d, c, half)]
        remote(rows, rows, wx_send.at[d, half], wx_recv.at[d, half], at_x(d)).wait_recv()

    to_sibling(0, 0)
    to_sibling(0, 1)

    pl.semaphore_wait(ready, 2)
    for copy in q_out[4:]:
        copy.start()

    for copy in k_out:
        copy.wait_recv()
    tiles = kt[...].astype(F32)
    tile_row = lax.broadcasted_iota(jnp.int32, (16, 128), 0)
    tile_lane = lax.broadcasted_iota(jnp.int32, (16, 128), 1)
    upper = jnp.where(tile_lane < 64, tiles[0], tiles[1])
    lower = jnp.where(tile_lane < 64, tiles[2], tiles[3])
    kr[pl.ds(z, 1)] = jnp.where(tile_row < 8, upper, lower).astype(BF)[None]
    kz_out, kf_out = [], []

    def at(d):
        return lax.rem(z + d + NZ, NZ)

    def key_hop(copies, n, d, source, rows):
        part = kl.at[rows, at(source)]
        copies.append(remote(part, part, kz_send.at[n, 0], kz_recv.at[n, 0], at_z(d)))
        if n != 7:
            part = kr.at[at(source)]
            copies.append(remote(part, part, kz_send.at[n, 1], kz_recv.at[n, 1], at_z(d)))

    every = slice(0, NY)
    for n, d in enumerate((2, 6, 1, 7)):
        key_hop(kz_out, n, d, 0, every)
    key_hop(kf_out, 4, 6, 2, slice(0, 2))
    key_hop(kf_out, 7, 2, -2, slice(2, 4))
    key_hop(kf_out, 5, 1, -2, every)
    key_hop(kf_out, 6, 7, 2, every)

    wf_out = []

    def pass_on(d, half):
        arrived(d, half)
        rows = w.at[half_rows(NX - d, c, half)]
        wf_out.append(remote(rows, rows, wf_send.at[half], wf_recv.at[half], at_x(d)))
        wf_out[-1].start()
        to_sibling(NX - d, half)

    owner_copy.wait()
    owner = owner_ref[0, 0]
    for copy in p_out:
        copy.wait_recv()
    chosen = p_recv[owner // NZ]
    chosen_rot = r_recv[owner // NZ]
    for k in range(NZ):
        z_send[k] = jnp.concatenate([chosen[k], chosen_rot[k % 2]], axis=1)
    pz_out = []
    for d in z_order:
        pz_out.append(remote(z_send.at[lax.rem(z + d, NZ)], z_recv.at[z], pz_send.at[d], pz_recv.at[d], at_z(d)))
    for copy in pz_out:
        copy.start()
    z_recv[pl.ds(z, 1)] = z_send[pl.ds(z, 1)]

    pass_on(1, 0)
    pass_on(3, 1)

    for copy in q_out:
        copy.wait_recv()

    def query_rows(dy, half):
        return qb.at[pl.ds(lax.rem(y + dy + NY, NY) * NZ + half * 4, 4)]

    qy_out, qf_out = [], []
    for step in range(2):
        for d in (1, 3):
            half = step if d == 1 else 1 - step
            part = query_rows(0, half)
            qy_out.append(remote(part, part, qy_send.at[d, half], qy_recv.at[d, half], at_y(d)))
    for copy in qy_out + kz_out:
        copy.start()

    for copy in pz_out:
        copy.wait_recv()
    pl_buf[pl.ds(y, 1), pl.ds(z, 1)] = z_recv[owner % NZ][None, None]
    pg_out = [remote(pl_buf.at[y, z], pl_buf.at[y, z], pg_send.at[d], pg_recv.at[d], at_z(d)) for d in z_order]
    for copy in pg_out:
        copy.start()
    for copy in kz_out:
        copy.wait_recv()
    for copy in kf_out:
        copy.start()
    for n, (d, half) in enumerate(((1, 0), (3, 1))):
        qy_out[n].wait_recv()
        part = query_rows(-1 if d == 1 else 1, half)
        qf_out.append(remote(part, part, qf_send.at[half], qf_recv.at[half], at_y(d)))
        qf_out[-1].start()

    arrived(1, 1)
    to_sibling(3, 1)
    arrived(3, 0)
    to_sibling(1, 0)
    for half in range(2):
        rows = w.at[half_rows(2, c, half)]
        remote(rows, rows, wf_send.at[half], wf_recv.at[half], sibling).wait_recv()
        to_sibling(2, half)

    for copy in pg_out:
        copy.wait_recv()
    py_out = []
    for d in y_order:
        part = pl_buf.at[y, :, :, 0:256]
        py_out.append(remote(part, part, py_send.at[d, 0], py_recv.at[d, 0], at_y(d)))
        part = pl_buf.at[y, 0:2, :, 256:384]
        py_out.append(remote(part, part, py_send.at[d, 1], py_recv.at[d, 1], at_y(d)))
    for copy in py_out:
        copy.start()

    for copy in qy_out[2:] + qf_out:
        copy.wait_recv()
    gathered = qb[...].astype(F32)
    x_buf[:, :768] = gathered[:, :8].reshape(TOK, 768).astype(BF)
    x_buf[:, 768:] = gathered[:, 8:].reshape(TOK, 768).astype(BF)
    for dx in range(NX):
        for half in range(2):
            from_sibling(dx, half)
    both = jnp.dot(x_buf[...], w[...], preferred_element_type=F32)
    plain[...] = both[:, :512].astype(BF)
    spun = both[:, 512:]
    lane = lax.broadcasted_iota(jnp.int32, (TOK, 256), 1)
    swapped = jnp.where(lane % 64 < 32, pltpu.roll(spun, 224, 1), pltpu.roll(spun, 32, 1))
    table_copy.wait()
    cosine = jnp.broadcast_to(table_ref[:16][None], (16, 16, 256)).reshape(TOK, 256)
    sine = jnp.broadcast_to(table_ref[16:][None], (16, 16, 256)).reshape(TOK, 256)
    turned[...] = (spun * cosine + swapped * sine).astype(BF)

    ku_copy.wait()
    for i in range(4):
        absorbed[i] = jnp.dot(
            plain[:, i * 128 : (i + 1) * 128], ku[i * 128 : (i + 1) * 128, :], preferred_element_type=F32
        ).astype(BF)

    for copy in kf_out:
        copy.wait_recv()
    gathered = kl[...].astype(F32).reshape(32, 16, 256)
    fresh[:, :256] = gathered[:, :8].reshape(TOK, 256).astype(BF)
    fresh[:, 256:] = gathered[:, 8:].reshape(TOK, 256).astype(BF)
    gathered = kr[...].astype(F32)
    rot_lane = lax.broadcasted_iota(jnp.int32, (64, 128), 1)
    for j in range(NY):
        piece = gathered[:, (j // 2) * 8 : (j // 2) * 8 + 8].reshape(64, 128)
        piece = jnp.where((rot_lane < 64) if j % 2 == 0 else (rot_lane >= 64), piece, 0.0)
        fresh_rot[j * 64 : (j + 1) * 64, :] = (piece + pltpu.roll(piece, 64, 1)).astype(BF)

    length_copy.wait()
    lengths = jnp.broadcast_to(length_ref[...], (TOK, 16))
    token = lax.broadcasted_iota(jnp.int32, (TOK, 16), 0)
    slot = lax.broadcasted_iota(jnp.int32, (TOK, 16), 1)
    limit = jnp.sum(jnp.where(token // RTOK == slot, lengths, 0).astype(F32), axis=1, keepdims=True)
    place = (lax.broadcasted_iota(jnp.int32, (TOK, 1), 0) % RTOK).astype(F32)
    live = place < limit

    t_half = lax.broadcasted_iota(jnp.int32, (128, 128), 0)
    s_half = lax.broadcasted_iota(jnp.int32, (128, 128), 1)
    allowed = (t_half // RTOK == s_half // RTOK) & (s_half <= t_half)
    pair_lane = lax.broadcasted_iota(jnp.int32, (TOK, 128), 1)

    def own_turned(i):
        mine_lanes = (pair_lane < 64) if i % 2 == 0 else (pair_lane >= 64)
        part = turned[:, (i // 2) * 128 : (i // 2 + 1) * 128].astype(F32)
        return jnp.where(mine_lanes, part, 0.0).astype(BF)

    for i in range(4):
        t = own_turned(i)
        for half in range(2):
            part = slice(half * 128, (half + 1) * 128)
            scores = dot_nt(absorbed[i, part, :], fresh[part, :]) + dot_nt(t[part], fresh_rot[part, :])
            own_buf[i, part, :] = jnp.where(allowed, scores, -jnp.inf)
    vu_copy.wait()

    for copy in py_out:
        copy.wait_recv()
    gathered = pl_buf[:, :, :, :256].astype(F32).reshape(32, 16, 256)
    latent[:, :256] = gathered[:, :8].reshape(PLEN, 256).astype(BF)
    latent[:, 256:] = gathered[:, 8:].reshape(PLEN, 256).astype(BF)
    for j in range(NY):
        both = jnp.concatenate([pl_buf[j, 0, :, 256:], pl_buf[j, 1, :, 256:]], axis=1)
        rotary[j * 16 : (j + 1) * 16, :] = both
        rotary[64 + j * 16 : 64 + (j + 1) * 16, :] = both

    for pair in range(2):
        outs = []
        for sub in range(2):
            i = pair * 2 + sub
            prompt_scores = dot_nt(absorbed[i], latent[...]) + jnp.dot(
                own_turned(i), rotary[...], preferred_element_type=F32
            )
            own_scores = own_buf[i]
            top = jnp.max(
                jnp.maximum(jnp.maximum(prompt_scores[:, :128], prompt_scores[:, 128:]), own_scores),
                axis=1,
                keepdims=True,
            )
            prompt_exp = jnp.exp2((prompt_scores - top) * (SCALE * LOG2E))
            own_exp = jnp.exp2((own_scores - top) * (SCALE * LOG2E))
            total = jnp.sum(prompt_exp[:, :128] + prompt_exp[:, 128:] + own_exp, axis=1, keepdims=True)
            factor = jnp.where(live, 1.0 / total, 0.0)
            own_weight = own_exp.astype(BF)
            mixed = jnp.dot(prompt_exp.astype(BF), latent[...], preferred_element_type=F32)
            mixed_own = jnp.concatenate(
                [
                    jnp.dot(own_weight[:128], fresh[:128, :], preferred_element_type=F32),
                    jnp.dot(own_weight[128:], fresh[128:, :], preferred_element_type=F32),
                ],
                axis=0,
            )
            mixed = ((mixed + mixed_own) * factor).astype(BF)
            out = jnp.dot(mixed, vu[:, i * 128 : (i + 1) * 128], preferred_element_type=F32)
            outs.append(out.reshape(32, 8, 128))
        o_send[pair] = jnp.concatenate(outs, axis=1).astype(BF)

        for dz in z_order + (0,):
            for dy in (2, 1, 3, 0):
                if dy or dz:
                    there = lax.rem(y + dy, NY) * NZ + lax.rem(z + dz, NZ)
                    remote(
                        o_send.at[pair, there], out_ref.at[h, pair], o_ssem.at[pair], o_rsem.at[pair], (g, there)
                    ).start()

        keep = pltpu.make_async_copy(o_send.at[pair, h], out_ref.at[h, pair], local_sem.at[5 + pair])
        keep.start()

    for copy in w_out + wf_out + wc_out + k_out + q_out + qy_out + qf_out + kz_out + kf_out + p_out + pz_out + pg_out + py_out:
        copy.wait_send()
    for pair in range(2):
        pltpu.make_async_copy(o_send.at[pair, h], out_ref.at[h, pair], local_sem.at[5 + pair]).wait()
        whole = remote(
            o_send.at[pair, pl.ds(0, 31)], out_ref.at[pl.ds(0, 31), pair], o_ssem.at[pair], o_rsem.at[pair], sibling
        )
        whole.wait_send()
        whole.wait_recv()


def local(
    query_latent, response_keys, prompt_cache, owners, lengths, w_query_plain, w_query_rotary, w_key_up, w_value_up
):
    vmem = pl.BlockSpec(memory_space=pltpu.VMEM)
    hbm = pl.BlockSpec(memory_space=pltpu.HBM)
    dma = pltpu.SemaphoreType.DMA
    gathered = pl.pallas_call(
        kernel,
        out_shape=jax.ShapeDtypeStruct((32, 2, 16, 128), BF),
        in_specs=[hbm] * 10,
        out_specs=hbm,
        scratch_shapes=[
            pltpu.SMEM((1, 1), jnp.int32),
            pltpu.VMEM((8, QLAT), BF),
            pltpu.VMEM((8, 576), BF),
            pltpu.VMEM((1, 16), jnp.int32),
            pltpu.VMEM((32, 256), F32),
            pltpu.VMEM((QLAT, 768), BF),
            pltpu.VMEM((512, 512), BF),
            pltpu.VMEM((512, 512), BF),
            pltpu.VMEM((1, 147456), BF),
            pltpu.VMEM((PLEN, 512), F32),
            pltpu.VMEM((16, 768), BF),
            pltpu.VMEM((16, 256), BF),
            pltpu.VMEM((16, 128), BF),
            pltpu.VMEM((32, 16, 768), BF),
            pltpu.VMEM((NY, NZ, 16, 256), BF),
            pltpu.VMEM((NY, 16, 128), BF),
            pltpu.VMEM((NZ, 16, 128), BF),
            pltpu.VMEM((NY, NZ, 16, 256), BF),
            pltpu.VMEM((NY, 2, 16, 128), BF),
            pltpu.VMEM((NY, NZ, 16, 256), BF),
            pltpu.VMEM((NY, 2, 16, 128), BF),
            pltpu.VMEM((NZ, 16, 384), BF),
            pltpu.VMEM((NZ, 16, 384), BF),
            pltpu.VMEM((NY, NZ, 16, 384), BF),
            pltpu.VMEM((TOK, QLAT), BF),
            pltpu.VMEM((TOK, 512), BF),
            pltpu.VMEM((TOK, 128), BF),
            pltpu.VMEM((PLEN, 512), BF),
            pltpu.VMEM((128, PLEN), BF),
            pltpu.VMEM((TOK, 512), BF),
            pltpu.VMEM((TOK, 256), BF),
            pltpu.VMEM((4, TOK, 512), BF),
            pltpu.VMEM((4, TOK, 128), F32),
            pltpu.VMEM((2, 32, 16, 128), BF),
            dma((12,)),
            *[dma((4, 2))] * 2,
            *[dma((2,))] * 2,
            *[dma((4, 2))] * 2,
            *[dma((8,))] * 2,
            *[dma((4, 2))] * 2,
            *[dma((2,))] * 2,
            *[dma((4, 2))] * 2,
            *[dma((8, 2))] * 2,
            *[dma((4, 2))] * 2,
            *[dma((8,))] * 4,
            *[dma((4, 2))] * 2,
            *[dma((2,))] * 2,
            pltpu.SemaphoreType.REGULAR,
        ],
        compiler_params=pltpu.CompilerParams(collective_id=0, has_side_effects=True, vmem_limit_bytes=60 << 20),
    )(
        owners.reshape(1, 1),
        query_latent,
        response_keys,
        lengths,
        jnp.asarray(rotary_tables()),
        prompt_cache,
        w_query_plain,
        w_query_rotary,
        w_key_up,
        w_value_up,
    )
    return gathered.reshape(32, 2, 2, 8, 128).transpose(3, 0, 1, 2, 4).reshape(8, 16384)


def solution(mesh):
    return jax.shard_map(
        local,
        mesh=mesh,
        in_specs=(
            P(("group", "head"), None),
            P(("group", "head"), None),
            P(("group", "head"), None),
            P("group"),
            P("group", None),
            P("group", "head"),
            P("group", "head"),
            P("head", None),
            P(None, "head"),
        ),
        out_specs=P(("group", "head"), None),
        check_vma=False,
    )
```

```python
import math

import jax
import jax.numpy as jnp
import numpy as np
from jax import lax
from jax.experimental import pallas as pl
from jax.experimental.pallas import tpu as pltpu
from jax.sharding import PartitionSpec as P

MESH = pl.DeviceIdType.MESH
LAT = 512
ROPE = 64
NOPE = 128
VDIM = 128
QLAT = 1536
PLEN = 256
RTOK = 16
TOK = 256
NX, NY, NZ = 4, 4, 8
SHARD = 192
HALF = 96
BF = jnp.bfloat16
F32 = jnp.float32
SCALE = 1.0 / math.sqrt(NOPE + ROPE)
LOG2E = 1.4426950408889634


def rotary_tables():
    position = (PLEN + np.arange(RTOK)).astype(np.float32)
    inverse = np.exp(np.arange(32).astype(np.float32) * np.float32(-2.0 * math.log(10000.0) / ROPE))
    angle = (position[:, None] * inverse[None, :].astype(np.float32)).astype(np.float32)
    cosine, sine = np.cos(angle), np.sin(angle)
    cos_table = np.tile(np.concatenate([cosine, cosine], 1), (1, 4))
    sin_table = np.tile(np.concatenate([-sine, sine], 1), (1, 4))
    return np.concatenate([cos_table, sin_table], 0).astype(np.float32)


def dot_nt(a, b):
    return lax.dot_general(a, b, (((1,), (1,)), ((), ())), preferred_element_type=F32)


def kernel(
    owner_hbm, query_hbm, keys_hbm, length_hbm, table_hbm, prompt_hbm, wp_hbm, wr_hbm, ku_hbm, vu_hbm,
    out_ref,
    owner_ref, query_ref, keys_ref, length_ref, table_ref, w, ku, vu, flat, stage, q_send, k_send, r_own, qb, kl, kt, kr,
    p_send, r_send, p_recv, r_recv, z_send, z_recv, pl_buf,
    x_buf, fresh, fresh_rot, latent, rotary, plain, turned, absorbed, own_buf, o_send,
    local_sem, wx_send, wx_recv, wf_send, wf_recv, wc_send, wc_recv,
    qz_send, qz_recv, qy_send, qy_recv, qf_send, qf_recv, ky_send, ky_recv, kz_send, kz_recv,
    pa_send, pa_recv, pz_send, pz_recv, pg_send, pg_recv, py_send, py_recv,
    o_ssem, o_rsem, ready,
):
    g = lax.axis_index("group")
    h = lax.axis_index("head")
    x, c = g // 2, g % 2
    y, z = h // NZ, h % NZ

    def at_x(d):
        return (lax.rem(x + d, NX) * 2 + c, h)

    def at_y(d):
        return (g, lax.rem(y + d, NY) * NZ + z)

    def at_z(d):
        return (g, y * NZ + lax.rem(z + d, NZ))

    sibling = (x * 2 + 1 - c, h)
    y_order = (1, 3, 2)
    z_far, z_near = (4, 3, 5), (2, 6, 1, 7)
    z_order = z_far + z_near

    def remote(src, dst, ssem, rsem, device):
        return pltpu.make_async_remote_copy(src, dst, ssem, rsem, device_id=device, device_id_type=MESH)

    barrier = pltpu.get_barrier_semaphore()
    peers = [sibling] + [at_x(d) for d in (1, 3)] + [at_y(d) for d in y_order] + [at_z(d) for d in z_near]
    for peer in peers:
        pl.semaphore_signal(barrier, inc=1, device_id=peer, device_id_type=MESH)

    def half_rows(dx, core, half):
        start = (lax.rem(x + dx + NX, NX) * 2 + core) * SHARD + half * HALF
        return pl.ds(pl.multiple_of(start, 32), HALF)

    mine = pl.ds(pl.multiple_of(g * SHARD, 64), SHARD)
    flat_copy = pltpu.make_async_copy(prompt_hbm, flat, local_sem.at[0])
    query_copy = pltpu.make_async_copy(query_hbm, query_ref, local_sem.at[7])
    keys_copy = pltpu.make_async_copy(keys_hbm, keys_ref, local_sem.at[8])
    wp_copy = pltpu.make_async_copy(wp_hbm, w.at[mine, 0:512], local_sem.at[3])
    wr_copy = pltpu.make_async_copy(wr_hbm, w.at[mine, 512:768], local_sem.at[4])
    owner_copy = pltpu.make_async_copy(owner_hbm, owner_ref, local_sem.at[9])
    length_copy = pltpu.make_async_copy(length_hbm, length_ref, local_sem.at[10])
    table_copy = pltpu.make_async_copy(table_hbm, table_ref, local_sem.at[11])
    ku_copy = pltpu.make_async_copy(ku_hbm, ku, local_sem.at[1])
    vu_copy = pltpu.make_async_copy(vu_hbm, vu, local_sem.at[2])
    for copy in (
        flat_copy, query_copy, keys_copy, wp_copy, wr_copy, owner_copy, length_copy, table_copy, ku_copy, vu_copy
    ):
        copy.start()

    flat_copy.wait()

    @pl.loop(0, PLEN // 8)
    def _(block):
        for r in range(8):
            row = flat[0:1, pl.ds(pl.multiple_of(block * 4096 + r * 512, 512), 512)].astype(F32)
            stage[pl.ds(block * 8 + r, 1), :] = row
        both = stage[pl.ds(pl.multiple_of(block * 8, 8), 8), :]
        p_send[pl.ds(block // 8, 1), pl.ds(block % 8, 1)] = jnp.concatenate(
            [both[:, :256], both[:, 256:]], axis=0
        ).astype(BF)[None, None]

    @pl.loop(0, NY)
    def _(j):
        for r in range(16):
            row = flat[0:1, pl.ds(pl.multiple_of(PLEN * LAT + j * 4096 + r * 256, 256), 256)].astype(F32)
            stage[pl.ds(r, 1), 0:256] = row
        both = stage[0:16, 0:256].astype(BF)
        r_send[pl.ds(j, 1), 0:1] = both[None, None, :, :128]
        r_send[pl.ds(j, 1), 1:2] = both[None, None, :, 128:]

    p_recv[pl.ds(y, 1)] = p_send[pl.ds(y, 1)]
    r_recv[pl.ds(y, 1)] = r_send[pl.ds(y, 1)]

    query_copy.wait()
    query = query_ref[...].astype(F32)
    packed = jnp.concatenate([query[:, :768], query[:, 768:]], axis=0).astype(BF)
    q_send[...] = packed
    qb[pl.ds(y, 1), 4:5] = packed[None, None]
    keys_copy.wait()
    keys = keys_ref[...].astype(F32)
    packed = jnp.concatenate([keys[:, :256], keys[:, 256:512]], axis=0).astype(BF)
    k_send[...] = packed
    kl[pl.ds(y, 1), pl.ds(z, 1)] = packed[None, None]
    rot = jnp.concatenate([keys[:, 512:], keys[:, 512:]], axis=1)
    packed = jnp.concatenate([rot, rot], axis=0).astype(BF)
    r_own[...] = packed
    kt[pl.ds(y, 1)] = packed[None]
    wp_copy.wait()
    wr_copy.wait()

    pl.semaphore_wait(barrier, len(peers))
    for d in (2, 6):
        pl.semaphore_signal(ready, inc=1, device_id=at_z(d), device_id_type=MESH)

    p_out, k_out = [], []
    for d in y_order:
        there = lax.rem(y + d, NY)
        k_out.append(remote(k_send, kl.at[y, z], ky_send.at[d, 0], ky_recv.at[d, 0], at_y(d)))
        k_out.append(remote(r_own, kt.at[y], ky_send.at[d, 1], ky_recv.at[d, 1], at_y(d)))
        p_out.append(remote(p_send.at[there], p_recv.at[y], pa_send.at[d, 0], pa_recv.at[d, 0], at_y(d)))
        p_out.append(remote(r_send.at[there], r_recv.at[y], pa_send.at[d, 1], pa_recv.at[d, 1], at_y(d)))
    q_out = [remote(q_send, qb.at[y, (12 - d) % NZ], qz_send.at[d], qz_recv.at[d], at_z(d)) for d in z_near + z_far]
    w_out = []
    for step in range(2):
        for d in (1, 3):
            half = step if d == 1 else 1 - step
            rows = w.at[half_rows(0, c, half)]
            w_out.append(remote(rows, rows, wx_send.at[d, half], wx_recv.at[d, half], at_x(d)))
    for copy in p_out + k_out + q_out[:4] + w_out:
        copy.start()
    wc_out = []

    def to_sibling(dx, half):
        rows = w.at[half_rows(dx, c, half)]
        wc_out.append(remote(rows, rows, wc_send.at[dx, half], wc_recv.at[dx, half], sibling))
        wc_out[-1].start()

    def from_sibling(dx, half):
        rows = w.at[half_rows(dx, 1 - c, half)]
        remote(rows, rows, wc_send.at[dx, half], wc_recv.at[dx, half], sibling).wait_recv()

    def arrived(d, half):
        rows = w.at[half_rows(NX - d, c, half)]
        remote(rows, rows, wx_send.at[d, half], wx_recv.at[d, half], at_x(d)).wait_recv()

    to_sibling(0, 0)
    to_sibling(0, 1)

    pl.semaphore_wait(ready, 2)
    for copy in q_out[4:]:
        copy.start()

    for copy in k_out:
        copy.wait_recv()
    tiles = kt[...].astype(F32)
    tile_row = lax.broadcasted_iota(jnp.int32, (16, 128), 0)
    tile_lane = lax.broadcasted_iota(jnp.int32, (16, 128), 1)
    upper = jnp.where(tile_lane < 64, tiles[0], tiles[1])
    lower = jnp.where(tile_lane < 64, tiles[2], tiles[3])
    kr[pl.ds(z, 1)] = jnp.where(tile_row < 8, upper, lower).astype(BF)[None]
    kz_out, kf_out = [], []

    def at(d):
        return lax.rem(z + d + NZ, NZ)

    def key_hop(copies, n, d, source, rows):
        part = kl.at[rows, at(source)]
        copies.append(remote(part, part, kz_send.at[n, 0], kz_recv.at[n, 0], at_z(d)))
        if n != 7:
            part = kr.at[at(source)]
            copies.append(remote(part, part, kz_send.at[n, 1], kz_recv.at[n, 1], at_z(d)))

    every = slice(0, NY)
    for n, d in enumerate((2, 6, 1, 7)):
        key_hop(kz_out, n, d, 0, every)
    key_hop(kf_out, 4, 6, 2, slice(0, 2))
    key_hop(kf_out, 7, 2, -2, slice(2, 4))
    key_hop(kf_out, 5, 1, -2, every)
    key_hop(kf_out, 6, 7, 2, every)

    wf_out = []

    def pass_on(d, half):
        arrived(d, half)
        rows = w.at[half_rows(NX - d, c, half)]
        wf_out.append(remote(rows, rows, wf_send.at[half], wf_recv.at[half], at_x(d)))
        wf_out[-1].start()
        to_sibling(NX - d, half)

    def query_hop(ssem, rsem, n, dy, first, last, d):
        part = qb.at[lax.rem(y + dy + NY, NY), first:last]
        return remote(part, part, ssem.at[d, n], rsem.at[d, n], at_y(d))

    for copy in q_out[:4]:
        copy.wait_recv()
    qy_near = [query_hop(qy_send, qy_recv, 0, 0, 2, 7, d) for d in (1, 3)]
    for copy in qy_near:
        copy.start()

    owner_copy.wait()
    owner = owner_ref[0, 0]
    for copy in p_out:
        copy.wait_recv()
    chosen = p_recv[owner // NZ]
    chosen_rot = r_recv[owner // NZ]
    for k in range(NZ):
        z_send[k] = jnp.concatenate([chosen[k], chosen_rot[k % 2]], axis=1)
    pz_out = []
    for d in z_order:
        pz_out.append(remote(z_send.at[lax.rem(z + d, NZ)], z_recv.at[z], pz_send.at[d], pz_recv.at[d], at_z(d)))
    for copy in pz_out:
        copy.start()
    z_recv[pl.ds(z, 1)] = z_send[pl.ds(z, 1)]

    pass_on(1, 0)
    pass_on(3, 1)

    for copy in q_out[4:]:
        copy.wait_recv()
    qy_far = [query_hop(qy_send, qy_recv, 1, 0, 0, 2, d) for d in (1, 3)]
    qy_far += [query_hop(qy_send, qy_recv, 2, 0, 7, 8, d) for d in (3, 1)]
    for copy in qy_far + kz_out:
        copy.start()
    for copy in qy_near:
        copy.wait_recv()
    qf_out = [query_hop(qf_send, qf_recv, 0, -1, 2, 5, 1), query_hop(qf_send, qf_recv, 0, 1, 5, 7, 3)]
    for copy in qf_out:
        copy.start()

    for copy in pz_out:
        copy.wait_recv()
    pl_buf[pl.ds(y, 1), 4:5] = z_recv[owner % NZ][None, None]
    pg_out = {}
    for d in z_order:
        pg_out[d] = remote(pl_buf.at[y, 4], pl_buf.at[y, (12 - d) % NZ], pg_send.at[d], pg_recv.at[d], at_z(d))
        pg_out[d].start()
    for copy in qy_far:
        copy.wait_recv()
    qf_far = [query_hop(qf_send, qf_recv, 1, 1, 0, 2, 3), query_hop(qf_send, qf_recv, 1, -1, 7, 8, 1)]
    for copy in qf_far:
        copy.start()
    for copy in kz_out:
        copy.wait_recv()
    for copy in kf_out:
        copy.start()
    arrived(1, 1)
    to_sibling(3, 1)
    arrived(3, 0)
    to_sibling(1, 0)
    for half in range(2):
        rows = w.at[half_rows(2, c, half)]
        remote(rows, rows, wf_send.at[half], wf_recv.at[half], sibling).wait_recv()
        to_sibling(2, half)

    py_out = []

    def spread_prompt(n, *index):
        part = pl_buf.at[(y, *index)]
        for d in y_order:
            py_out.append(remote(part, part, py_send.at[d, n], py_recv.at[d, n], at_y(d)))
            py_out[-1].start()

    for d in z_near:
        pg_out[d].wait_recv()
    spread_prompt(0, slice(2, 7), slice(None), slice(0, 256))
    spread_prompt(1, slice(4, 6), slice(None), slice(256, 384))
    for d in z_far:
        pg_out[d].wait_recv()
    spread_prompt(2, slice(0, 2), slice(None), slice(0, 256))
    spread_prompt(3, slice(7, 8), slice(None), slice(0, 256))

    for copy in qf_out + qf_far:
        copy.wait_recv()
    for j in range(NY):
        gathered = jnp.concatenate(
            [qb[pl.ds(j, 1), pl.ds(lax.rem(k - z + 12, NZ), 1)].astype(F32)[0] for k in range(NZ)], axis=0
        )
        x_buf[j * 64 : (j + 1) * 64, :768] = gathered[:, :8].reshape(64, 768).astype(BF)
        x_buf[j * 64 : (j + 1) * 64, 768:] = gathered[:, 8:].reshape(64, 768).astype(BF)
    for dx in range(NX):
        for half in range(2):
            from_sibling(dx, half)
    both = jnp.dot(x_buf[...], w[...], preferred_element_type=F32)
    plain[...] = both[:, :512].astype(BF)
    spun = both[:, 512:]
    lane = lax.broadcasted_iota(jnp.int32, (TOK, 256), 1)
    swapped = jnp.where(lane % 64 < 32, pltpu.roll(spun, 224, 1), pltpu.roll(spun, 32, 1))
    table_copy.wait()
    cosine = jnp.broadcast_to(table_ref[:16][None], (16, 16, 256)).reshape(TOK, 256)
    sine = jnp.broadcast_to(table_ref[16:][None], (16, 16, 256)).reshape(TOK, 256)
    turned[...] = (spun * cosine + swapped * sine).astype(BF)

    ku_copy.wait()
    for i in range(4):
        absorbed[i] = jnp.dot(
            plain[:, i * 128 : (i + 1) * 128], ku[i * 128 : (i + 1) * 128, :], preferred_element_type=F32
        ).astype(BF)

    for copy in kf_out:
        copy.wait_recv()
    gathered = kl[...].astype(F32).reshape(32, 16, 256)
    fresh[:, :256] = gathered[:, :8].reshape(TOK, 256).astype(BF)
    fresh[:, 256:] = gathered[:, 8:].reshape(TOK, 256).astype(BF)
    gathered = kr[...].astype(F32)
    rot_lane = lax.broadcasted_iota(jnp.int32, (64, 128), 1)
    for j in range(NY):
        piece = gathered[:, (j // 2) * 8 : (j // 2) * 8 + 8].reshape(64, 128)
        piece = jnp.where((rot_lane < 64) if j % 2 == 0 else (rot_lane >= 64), piece, 0.0)
        fresh_rot[j * 64 : (j + 1) * 64, :] = (piece + pltpu.roll(piece, 64, 1)).astype(BF)

    length_copy.wait()
    lengths = jnp.broadcast_to(length_ref[...], (TOK, 16))
    token = lax.broadcasted_iota(jnp.int32, (TOK, 16), 0)
    slot = lax.broadcasted_iota(jnp.int32, (TOK, 16), 1)
    limit = jnp.sum(jnp.where(token // RTOK == slot, lengths, 0).astype(F32), axis=1, keepdims=True)
    place = (lax.broadcasted_iota(jnp.int32, (TOK, 1), 0) % RTOK).astype(F32)
    live = place < limit

    t_half = lax.broadcasted_iota(jnp.int32, (128, 128), 0)
    s_half = lax.broadcasted_iota(jnp.int32, (128, 128), 1)
    allowed = (t_half // RTOK == s_half // RTOK) & (s_half <= t_half)
    pair_lane = lax.broadcasted_iota(jnp.int32, (TOK, 128), 1)

    def own_turned(i):
        mine_lanes = (pair_lane < 64) if i % 2 == 0 else (pair_lane >= 64)
        part = turned[:, (i // 2) * 128 : (i // 2 + 1) * 128].astype(F32)
        return jnp.where(mine_lanes, part, 0.0).astype(BF)

    for i in range(4):
        t = own_turned(i)
        for half in range(2):
            part = slice(half * 128, (half + 1) * 128)
            scores = dot_nt(absorbed[i, part, :], fresh[part, :]) + dot_nt(t[part], fresh_rot[part, :])
            own_buf[i, part, :] = jnp.where(allowed, scores, -jnp.inf)
    vu_copy.wait()

    for copy in py_out:
        copy.wait_recv()
    gathered = pl_buf[:, :, :, :256].astype(F32).reshape(32, 16, 256)
    latent[:, :256] = gathered[:, :8].reshape(PLEN, 256).astype(BF)
    latent[:, 256:] = gathered[:, 8:].reshape(PLEN, 256).astype(BF)
    tiles = []
    for j in range(NY):
        tiles.append(
            jnp.concatenate(
                [pl_buf[pl.ds(j, 1), pl.ds(4 + lax.rem(z + n, 2), 1), :, 256:].astype(F32)[0, 0] for n in range(2)], axis=1
            )
        )
    tiles = jnp.concatenate(tiles, axis=0)
    turn = lax.rem(z + 4, NZ) * 8
    key_lane = lax.broadcasted_iota(jnp.int32, (ROPE, PLEN), 1) % 64
    tiles = jnp.where(
        key_lane < 64 - turn, pltpu.roll(tiles, lax.rem(PLEN - turn, PLEN), 1), pltpu.roll(tiles, 64 - turn, 1)
    ).astype(BF)
    rotary[:64, :] = tiles
    rotary[64:, :] = tiles

    for pair in range(2):
        outs = []
        for sub in range(2):
            i = pair * 2 + sub
            prompt_scores = dot_nt(absorbed[i], latent[...]) + jnp.dot(
                own_turned(i), rotary[...], preferred_element_type=F32
            )
            own_scores = own_buf[i]
            top = jnp.max(
                jnp.maximum(jnp.maximum(prompt_scores[:, :128], prompt_scores[:, 128:]), own_scores),
                axis=1,
                keepdims=True,
            )
            prompt_exp = jnp.exp2((prompt_scores - top) * (SCALE * LOG2E))
            own_exp = jnp.exp2((own_scores - top) * (SCALE * LOG2E))
            total = jnp.sum(prompt_exp[:, :128] + prompt_exp[:, 128:] + own_exp, axis=1, keepdims=True)
            factor = jnp.where(live, 1.0 / total, 0.0)
            own_weight = own_exp.astype(BF)
            mixed = jnp.dot(prompt_exp.astype(BF), latent[...], preferred_element_type=F32)
            mixed_own = jnp.concatenate(
                [
                    jnp.dot(own_weight[:128], fresh[:128, :], preferred_element_type=F32),
                    jnp.dot(own_weight[128:], fresh[128:, :], preferred_element_type=F32),
                ],
                axis=0,
            )
            mixed = ((mixed + mixed_own) * factor).astype(BF)
            out = jnp.dot(mixed, vu[:, i * 128 : (i + 1) * 128], preferred_element_type=F32)
            outs.append(out.reshape(32, 8, 128))
        o_send[pair] = jnp.concatenate(outs, axis=1).astype(BF)

        for dz in z_order + (0,):
            for dy in (2, 1, 3, 0):
                if dy or dz:
                    there = lax.rem(y + dy, NY) * NZ + lax.rem(z + dz, NZ)
                    remote(
                        o_send.at[pair, there], out_ref.at[h, pair], o_ssem.at[pair], o_rsem.at[pair], (g, there)
                    ).start()

        keep = pltpu.make_async_copy(o_send.at[pair, h], out_ref.at[h, pair], local_sem.at[5 + pair])
        keep.start()

    for copy in w_out + wf_out + wc_out + k_out + q_out + qy_near + qy_far + qf_out + qf_far + kz_out + kf_out + p_out + pz_out + list(pg_out.values()) + py_out:
        copy.wait_send()
    for pair in range(2):
        pltpu.make_async_copy(o_send.at[pair, h], out_ref.at[h, pair], local_sem.at[5 + pair]).wait()
        whole = remote(
            o_send.at[pair, pl.ds(0, 31)], out_ref.at[pl.ds(0, 31), pair], o_ssem.at[pair], o_rsem.at[pair], sibling
        )
        whole.wait_send()
        whole.wait_recv()


def local(
    query_latent, response_keys, prompt_cache, owners, lengths, w_query_plain, w_query_rotary, w_key_up, w_value_up
):
    vmem = pl.BlockSpec(memory_space=pltpu.VMEM)
    hbm = pl.BlockSpec(memory_space=pltpu.HBM)
    dma = pltpu.SemaphoreType.DMA
    gathered = pl.pallas_call(
        kernel,
        out_shape=jax.ShapeDtypeStruct((32, 2, 16, 128), BF),
        in_specs=[hbm] * 10,
        out_specs=hbm,
        scratch_shapes=[
            pltpu.SMEM((1, 1), jnp.int32),
            pltpu.VMEM((8, QLAT), BF),
            pltpu.VMEM((8, 576), BF),
            pltpu.VMEM((1, 16), jnp.int32),
            pltpu.VMEM((32, 256), F32),
            pltpu.VMEM((QLAT, 768), BF),
            pltpu.VMEM((512, 512), BF),
            pltpu.VMEM((512, 512), BF),
            pltpu.VMEM((1, 147456), BF),
            pltpu.VMEM((PLEN, 512), F32),
            pltpu.VMEM((16, 768), BF),
            pltpu.VMEM((16, 256), BF),
            pltpu.VMEM((16, 128), BF),
            pltpu.VMEM((NY, NZ, 16, 768), BF),
            pltpu.VMEM((NY, NZ, 16, 256), BF),
            pltpu.VMEM((NY, 16, 128), BF),
            pltpu.VMEM((NZ, 16, 128), BF),
            pltpu.VMEM((NY, NZ, 16, 256), BF),
            pltpu.VMEM((NY, 2, 16, 128), BF),
            pltpu.VMEM((NY, NZ, 16, 256), BF),
            pltpu.VMEM((NY, 2, 16, 128), BF),
            pltpu.VMEM((NZ, 16, 384), BF),
            pltpu.VMEM((NZ, 16, 384), BF),
            pltpu.VMEM((NY, NZ, 16, 384), BF),
            pltpu.VMEM((TOK, QLAT), BF),
            pltpu.VMEM((TOK, 512), BF),
            pltpu.VMEM((TOK, 128), BF),
            pltpu.VMEM((PLEN, 512), BF),
            pltpu.VMEM((128, PLEN), BF),
            pltpu.VMEM((TOK, 512), BF),
            pltpu.VMEM((TOK, 256), BF),
            pltpu.VMEM((4, TOK, 512), BF),
            pltpu.VMEM((4, TOK, 128), F32),
            pltpu.VMEM((2, 32, 16, 128), BF),
            dma((12,)),
            *[dma((4, 2))] * 2,
            *[dma((2,))] * 2,
            *[dma((4, 2))] * 2,
            *[dma((8,))] * 2,
            *[dma((4, 3))] * 2,
            *[dma((4, 2))] * 2,
            *[dma((4, 2))] * 2,
            *[dma((8, 2))] * 2,
            *[dma((4, 2))] * 2,
            *[dma((8,))] * 4,
            *[dma((4, 4))] * 2,
            *[dma((2,))] * 2,
            pltpu.SemaphoreType.REGULAR,
        ],
        compiler_params=pltpu.CompilerParams(collective_id=0, has_side_effects=True, vmem_limit_bytes=60 << 20),
    )(
        owners.reshape(1, 1),
        query_latent,
        response_keys,
        lengths,
        jnp.asarray(rotary_tables()),
        prompt_cache,
        w_query_plain,
        w_query_rotary,
        w_key_up,
        w_value_up,
    )
    return gathered.reshape(32, 2, 2, 8, 128).transpose(3, 0, 1, 2, 4).reshape(8, 16384)


def solution(mesh):
    return jax.shard_map(
        local,
        mesh=mesh,
        in_specs=(
            P(("group", "head"), None),
            P(("group", "head"), None),
            P(("group", "head"), None),
            P("group"),
            P("group", None),
            P("group", "head"),
            P("group", "head"),
            P("head", None),
            P(None, "head"),
        ),
        out_specs=P(("group", "head"), None),
        check_vma=False,
    )
```

```python
import math

import jax
import jax.numpy as jnp
import numpy as np
from jax import lax
from jax.experimental import pallas as pl
from jax.experimental.pallas import tpu as pltpu
from jax.sharding import PartitionSpec as P

MESH = pl.DeviceIdType.MESH
LAT = 512
ROPE = 64
NOPE = 128
VDIM = 128
QLAT = 1536
PLEN = 256
RTOK = 16
TOK = 256
NX, NY, NZ = 4, 4, 8
SHARD = 192
HALF = 96
BF = jnp.bfloat16
F32 = jnp.float32
SCALE = 1.0 / math.sqrt(NOPE + ROPE)
LOG2E = 1.4426950408889634


def rotary_tables():
    position = (PLEN + np.arange(RTOK)).astype(np.float32)
    inverse = np.exp(np.arange(32).astype(np.float32) * np.float32(-2.0 * math.log(10000.0) / ROPE))
    angle = (position[:, None] * inverse[None, :].astype(np.float32)).astype(np.float32)
    cosine, sine = np.cos(angle), np.sin(angle)
    cos_table = np.tile(np.concatenate([cosine, cosine], 1), (1, 4))
    sin_table = np.tile(np.concatenate([-sine, sine], 1), (1, 4))
    return np.concatenate([cos_table, sin_table], 0).astype(np.float32)


def dot_nt(a, b):
    return lax.dot_general(a, b, (((1,), (1,)), ((), ())), preferred_element_type=F32)


def kernel(
    owner_hbm, query_hbm, keys_hbm, length_hbm, table_hbm, prompt_hbm, wp_hbm, wr_hbm, ku_hbm, vu_hbm,
    out_ref,
    owner_ref, query_ref, keys_ref, length_ref, table_ref, w, ku, vu, flat, stage, q_send, k_send, r_own, qb, kl, kt, kr,
    p_send, r_send, p_recv, r_recv, z_send, z_recv, pl_buf,
    x_buf, fresh, fresh_rot, latent, rotary, plain, turned, absorbed, own_buf, o_send,
    local_sem, wx_send, wx_recv, wf_send, wf_recv, wc_send, wc_recv,
    qz_send, qz_recv, qy_send, qy_recv, qf_send, qf_recv, ky_send, ky_recv, kz_send, kz_recv,
    pa_send, pa_recv, pz_send, pz_recv, pg_send, pg_recv, py_send, py_recv,
    o_ssem, o_rsem, ready,
):
    g = lax.axis_index("group")
    h = lax.axis_index("head")
    x, c = g // 2, g % 2
    y, z = h // NZ, h % NZ

    def at_x(d):
        return (lax.rem(x + d, NX) * 2 + c, h)

    def at_y(d):
        return (g, lax.rem(y + d, NY) * NZ + z)

    def at_z(d):
        return (g, y * NZ + lax.rem(z + d, NZ))

    sibling = (x * 2 + 1 - c, h)
    y_order = (1, 3, 2)
    z_far, z_near = (4, 3, 5), (2, 6, 1, 7)
    z_order = z_far + z_near

    def remote(src, dst, ssem, rsem, device):
        return pltpu.make_async_remote_copy(src, dst, ssem, rsem, device_id=device, device_id_type=MESH)

    barrier = pltpu.get_barrier_semaphore()
    peers = [sibling] + [at_x(d) for d in (1, 3)] + [at_y(d) for d in y_order] + [at_z(d) for d in z_near]
    for peer in peers:
        pl.semaphore_signal(barrier, inc=1, device_id=peer, device_id_type=MESH)

    def half_rows(dx, core, half):
        start = (lax.rem(x + dx + NX, NX) * 2 + core) * SHARD + half * HALF
        return pl.ds(pl.multiple_of(start, 32), HALF)

    mine = pl.ds(pl.multiple_of(g * SHARD, 64), SHARD)
    flat_copy = pltpu.make_async_copy(prompt_hbm, flat, local_sem.at[0])
    query_copy = pltpu.make_async_copy(query_hbm, query_ref, local_sem.at[7])
    keys_copy = pltpu.make_async_copy(keys_hbm, keys_ref, local_sem.at[8])
    wp_copy = pltpu.make_async_copy(wp_hbm, w.at[mine, 0:512], local_sem.at[3])
    wr_copy = pltpu.make_async_copy(wr_hbm, w.at[mine, 512:768], local_sem.at[4])
    owner_copy = pltpu.make_async_copy(owner_hbm, owner_ref, local_sem.at[9])
    length_copy = pltpu.make_async_copy(length_hbm, length_ref, local_sem.at[10])
    table_copy = pltpu.make_async_copy(table_hbm, table_ref, local_sem.at[11])
    ku_copy = pltpu.make_async_copy(ku_hbm, ku, local_sem.at[1])
    vu_copy = pltpu.make_async_copy(vu_hbm, vu, local_sem.at[2])
    for copy in (
        flat_copy, query_copy, keys_copy, wp_copy, wr_copy, owner_copy, length_copy, table_copy, ku_copy, vu_copy
    ):
        copy.start()

    flat_copy.wait()

    @pl.loop(0, PLEN // 8)
    def _(block):
        for r in range(8):
            row = flat[0:1, pl.ds(pl.multiple_of(block * 4096 + r * 512, 512), 512)].astype(F32)
            stage[pl.ds(block * 8 + r, 1), :] = row
        both = stage[pl.ds(pl.multiple_of(block * 8, 8), 8), :]
        p_send[pl.ds(block // 8, 1), pl.ds(block % 8, 1)] = jnp.concatenate(
            [both[:, :256], both[:, 256:]], axis=0
        ).astype(BF)[None, None]

    @pl.loop(0, NY)
    def _(j):
        for r in range(16):
            row = flat[0:1, pl.ds(pl.multiple_of(PLEN * LAT + j * 4096 + r * 256, 256), 256)].astype(F32)
            stage[pl.ds(r, 1), 0:256] = row
        both = stage[0:16, 0:256].astype(BF)
        r_send[pl.ds(j, 1), 0:1] = both[None, None, :, :128]
        r_send[pl.ds(j, 1), 1:2] = both[None, None, :, 128:]

    p_recv[pl.ds(y, 1)] = p_send[pl.ds(y, 1)]
    r_recv[pl.ds(y, 1)] = r_send[pl.ds(y, 1)]

    query_copy.wait()
    query = query_ref[...].astype(F32)
    packed = jnp.concatenate([query[:, :768], query[:, 768:]], axis=0).astype(BF)
    q_send[...] = packed
    qb[pl.ds(y, 1), 4:5] = packed[None, None]
    keys_copy.wait()
    keys = keys_ref[...].astype(F32)
    packed = jnp.concatenate([keys[:, :256], keys[:, 256:512]], axis=0).astype(BF)
    k_send[...] = packed
    kl[pl.ds(y, 1), pl.ds(z, 1)] = packed[None, None]
    rot = jnp.concatenate([keys[:, 512:], keys[:, 512:]], axis=1)
    packed = jnp.concatenate([rot, rot], axis=0).astype(BF)
    r_own[...] = packed
    kt[pl.ds(y, 1)] = packed[None]
    wp_copy.wait()
    wr_copy.wait()

    pl.semaphore_wait(barrier, len(peers))
    for d in (2, 6):
        pl.semaphore_signal(ready, inc=1, device_id=at_z(d), device_id_type=MESH)

    p_out, k_out = [], []
    for d in y_order:
        there = lax.rem(y + d, NY)
        k_out.append(remote(k_send, kl.at[y, z], ky_send.at[d, 0], ky_recv.at[d, 0], at_y(d)))
        k_out.append(remote(r_own, kt.at[y], ky_send.at[d, 1], ky_recv.at[d, 1], at_y(d)))
        p_out.append(remote(p_send.at[there], p_recv.at[y], pa_send.at[d, 0], pa_recv.at[d, 0], at_y(d)))
        p_out.append(remote(r_send.at[there], r_recv.at[y], pa_send.at[d, 1], pa_recv.at[d, 1], at_y(d)))
    q_out = [remote(q_send, qb.at[y, (12 - d) % NZ], qz_send.at[d], qz_recv.at[d], at_z(d)) for d in z_near + z_far]
    w_out = []
    for step in range(2):
        for d in (1, 3):
            half = step if d == 1 else 1 - step
            rows = w.at[half_rows(0, c, half)]
            w_out.append(remote(rows, rows, wx_send.at[d, half], wx_recv.at[d, half], at_x(d)))
    for copy in p_out + k_out + q_out[:4] + w_out:
        copy.start()
    wc_out = []

    def to_sibling(dx, half):
        rows = w.at[half_rows(dx, c, half)]
        wc_out.append(remote(rows, rows, wc_send.at[dx, half], wc_recv.at[dx, half], sibling))
        wc_out[-1].start()

    def from_sibling(dx, half):
        rows = w.at[half_rows(dx, 1 - c, half)]
        remote(rows, rows, wc_send.at[dx, half], wc_recv.at[dx, half], sibling).wait_recv()

    def arrived(d, half):
        rows = w.at[half_rows(NX - d, c, half)]
        remote(rows, rows, wx_send.at[d, half], wx_recv.at[d, half], at_x(d)).wait_recv()

    to_sibling(0, 0)
    to_sibling(0, 1)

    pl.semaphore_wait(ready, 2)
    for copy in q_out[4:]:
        copy.start()

    for copy in k_out:
        copy.wait_recv()
    tiles = kt[...].astype(F32)
    tile_row = lax.broadcasted_iota(jnp.int32, (16, 128), 0)
    tile_lane = lax.broadcasted_iota(jnp.int32, (16, 128), 1)
    upper = jnp.where(tile_lane < 64, tiles[0], tiles[1])
    lower = jnp.where(tile_lane < 64, tiles[2], tiles[3])
    kr[pl.ds(z, 1)] = jnp.where(tile_row < 8, upper, lower).astype(BF)[None]
    kz_out, kf_out = [], []

    def at(d):
        return lax.rem(z + d + NZ, NZ)

    def key_hop(copies, n, d, source, rows):
        part = kl.at[rows, at(source)]
        copies.append(remote(part, part, kz_send.at[n, 0], kz_recv.at[n, 0], at_z(d)))
        if n != 7:
            part = kr.at[at(source)]
            copies.append(remote(part, part, kz_send.at[n, 1], kz_recv.at[n, 1], at_z(d)))

    every = slice(0, NY)
    for n, d in enumerate((2, 6, 1, 7)):
        key_hop(kz_out, n, d, 0, every)
    key_hop(kf_out, 4, 6, 2, slice(0, 2))
    key_hop(kf_out, 7, 2, -2, slice(2, 4))
    key_hop(kf_out, 5, 1, -2, every)
    key_hop(kf_out, 6, 7, 2, every)

    wf_out = []

    def pass_on(d, half):
        arrived(d, half)
        rows = w.at[half_rows(NX - d, c, half)]
        wf_out.append(remote(rows, rows, wf_send.at[half], wf_recv.at[half], at_x(d)))
        wf_out[-1].start()
        to_sibling(NX - d, half)

    def query_hop(ssem, rsem, n, dy, first, last, d):
        part = qb.at[lax.rem(y + dy + NY, NY), first:last]
        return remote(part, part, ssem.at[d, n], rsem.at[d, n], at_y(d))

    for copy in q_out[:4]:
        copy.wait_recv()
    qy_near = [query_hop(qy_send, qy_recv, 0, 0, 2, 7, d) for d in (1, 3)]
    for copy in qy_near:
        copy.start()

    owner_copy.wait()
    owner = owner_ref[0, 0]
    for copy in p_out:
        copy.wait_recv()
    chosen = p_recv[owner // NZ]
    chosen_rot = r_recv[owner // NZ]
    for k in range(NZ):
        z_send[k] = jnp.concatenate([chosen[k], chosen_rot[k % 2]], axis=1)
    pz_out = []
    for d in z_order:
        pz_out.append(remote(z_send.at[lax.rem(z + d, NZ)], z_recv.at[z], pz_send.at[d], pz_recv.at[d], at_z(d)))
    for copy in pz_out:
        copy.start()
    z_recv[pl.ds(z, 1)] = z_send[pl.ds(z, 1)]

    pass_on(1, 0)
    pass_on(3, 1)

    for copy in q_out[4:]:
        copy.wait_recv()
    qy_far = [query_hop(qy_send, qy_recv, 1, 0, 0, 2, d) for d in (1, 3)]
    qy_far += [query_hop(qy_send, qy_recv, 2, 0, 7, 8, d) for d in (3, 1)]
    for copy in qy_far + kz_out:
        copy.start()
    for copy in qy_near:
        copy.wait_recv()
    qf_out = [query_hop(qf_send, qf_recv, 0, -1, 2, 5, 1), query_hop(qf_send, qf_recv, 0, 1, 5, 7, 3)]
    for copy in qf_out:
        copy.start()

    for copy in pz_out:
        copy.wait_recv()
    pl_buf[pl.ds(y, 1), 4:5] = z_recv[owner % NZ][None, None]
    pg_out = {}
    for d in z_order:
        pg_out[d] = remote(pl_buf.at[y, 4], pl_buf.at[y, (12 - d) % NZ], pg_send.at[d], pg_recv.at[d], at_z(d))
        pg_out[d].start()
    for copy in qy_far:
        copy.wait_recv()
    qf_far = [query_hop(qf_send, qf_recv, 1, 1, 0, 2, 3), query_hop(qf_send, qf_recv, 1, -1, 7, 8, 1)]
    for copy in qf_far:
        copy.start()
    for copy in kz_out:
        copy.wait_recv()
    for copy in kf_out:
        copy.start()
    arrived(1, 1)
    to_sibling(3, 1)
    arrived(3, 0)
    to_sibling(1, 0)
    for half in range(2):
        rows = w.at[half_rows(2, c, half)]
        remote(rows, rows, wf_send.at[half], wf_recv.at[half], sibling).wait_recv()
        to_sibling(2, half)

    py_out = []

    def spread_prompt(n, *index):
        part = pl_buf.at[(y, *index)]
        for d in y_order:
            py_out.append(remote(part, part, py_send.at[d, n], py_recv.at[d, n], at_y(d)))
            py_out[-1].start()

    for d in z_near:
        pg_out[d].wait_recv()
    spread_prompt(0, slice(2, 7), slice(None), slice(0, 256))
    spread_prompt(1, slice(4, 6), slice(None), slice(256, 384))
    for d in z_far:
        pg_out[d].wait_recv()
    spread_prompt(2, slice(0, 2), slice(None), slice(0, 256))
    spread_prompt(3, slice(7, 8), slice(None), slice(0, 256))

    for copy in qf_out + qf_far:
        copy.wait_recv()
    for j in range(NY):
        gathered = jnp.concatenate(
            [qb[pl.ds(j, 1), pl.ds(lax.rem(k - z + 12, NZ), 1)].astype(F32)[0] for k in range(NZ)], axis=0
        )
        x_buf[j * 64 : (j + 1) * 64, :768] = gathered[:, :8].reshape(64, 768).astype(BF)
        x_buf[j * 64 : (j + 1) * 64, 768:] = gathered[:, 8:].reshape(64, 768).astype(BF)
    for dx in range(NX):
        for half in range(2):
            from_sibling(dx, half)
    both = jnp.dot(x_buf[...], w[...], preferred_element_type=F32)
    plain[...] = both[:, :512].astype(BF)
    spun = both[:, 512:]
    lane = lax.broadcasted_iota(jnp.int32, (TOK, 256), 1)
    swapped = jnp.where(lane % 64 < 32, pltpu.roll(spun, 224, 1), pltpu.roll(spun, 32, 1))
    table_copy.wait()
    cosine = jnp.broadcast_to(table_ref[:16][None], (16, 16, 256)).reshape(TOK, 256)
    sine = jnp.broadcast_to(table_ref[16:][None], (16, 16, 256)).reshape(TOK, 256)
    turned[...] = (spun * cosine + swapped * sine).astype(BF)

    ku_copy.wait()
    for i in range(4):
        absorbed[i] = jnp.dot(
            plain[:, i * 128 : (i + 1) * 128], ku[i * 128 : (i + 1) * 128, :], preferred_element_type=F32
        ).astype(BF)

    for copy in kf_out:
        copy.wait_recv()
    gathered = kl[...].astype(F32).reshape(32, 16, 256)
    fresh[:, :256] = gathered[:, :8].reshape(TOK, 256).astype(BF)
    fresh[:, 256:] = gathered[:, 8:].reshape(TOK, 256).astype(BF)
    gathered = kr[...].astype(F32)
    rot_lane = lax.broadcasted_iota(jnp.int32, (64, 128), 1)
    for j in range(NY):
        piece = gathered[:, (j // 2) * 8 : (j // 2) * 8 + 8].reshape(64, 128)
        piece = jnp.where((rot_lane < 64) if j % 2 == 0 else (rot_lane >= 64), piece, 0.0)
        fresh_rot[j * 64 : (j + 1) * 64, :] = (piece + pltpu.roll(piece, 64, 1)).astype(BF)

    length_copy.wait()
    lengths = jnp.broadcast_to(length_ref[...], (TOK, 16))
    token = lax.broadcasted_iota(jnp.int32, (TOK, 16), 0)
    slot = lax.broadcasted_iota(jnp.int32, (TOK, 16), 1)
    limit = jnp.sum(jnp.where(token // RTOK == slot, lengths, 0).astype(F32), axis=1, keepdims=True)
    place = (lax.broadcasted_iota(jnp.int32, (TOK, 1), 0) % RTOK).astype(F32)
    live = place < limit

    t_half = lax.broadcasted_iota(jnp.int32, (128, 128), 0)
    s_half = lax.broadcasted_iota(jnp.int32, (128, 128), 1)
    allowed = (t_half // RTOK == s_half // RTOK) & (s_half <= t_half)
    pair_lane = lax.broadcasted_iota(jnp.int32, (TOK, 128), 1)

    def own_turned(i):
        mine_lanes = (pair_lane < 64) if i % 2 == 0 else (pair_lane >= 64)
        part = turned[:, (i // 2) * 128 : (i // 2 + 1) * 128].astype(F32)
        return jnp.where(mine_lanes, part, 0.0).astype(BF)

    for half in range(2):
        part = slice(half * 128, (half + 1) * 128)
        a = absorbed[:, part, :].reshape(512, LAT)
        t = jnp.concatenate([own_turned(i)[part] for i in range(4)], axis=0)
        scores = dot_nt(a, fresh[part, :]) + dot_nt(t, fresh_rot[part, :])
        own_buf[:, part, :] = jnp.where(allowed[None], scores.reshape(4, 128, 128), -jnp.inf)
    vu_copy.wait()

    for copy in py_out:
        copy.wait_recv()
    gathered = pl_buf[:, :, :, :256].astype(F32).reshape(32, 16, 256)
    latent[:, :256] = gathered[:, :8].reshape(PLEN, 256).astype(BF)
    latent[:, 256:] = gathered[:, 8:].reshape(PLEN, 256).astype(BF)
    tiles = []
    for j in range(NY):
        tiles.append(
            jnp.concatenate(
                [pl_buf[pl.ds(j, 1), pl.ds(4 + lax.rem(z + n, 2), 1), :, 256:].astype(F32)[0, 0] for n in range(2)], axis=1
            )
        )
    tiles = jnp.concatenate(tiles, axis=0)
    turn = lax.rem(z + 4, NZ) * 8
    key_lane = lax.broadcasted_iota(jnp.int32, (ROPE, PLEN), 1) % 64
    tiles = jnp.where(
        key_lane < 64 - turn, pltpu.roll(tiles, lax.rem(PLEN - turn, PLEN), 1), pltpu.roll(tiles, 64 - turn, 1)
    ).astype(BF)
    rotary[:64, :] = tiles
    rotary[64:, :] = tiles

    latent_t = latent[...].T
    for pair in range(2):
        a = absorbed[pair * 2 : pair * 2 + 2].reshape(512, LAT)
        t = jnp.concatenate([own_turned(pair * 2), own_turned(pair * 2 + 1)], axis=0)
        prompt_scores = jnp.dot(a, latent_t, preferred_element_type=F32) + jnp.dot(t, rotary[...], preferred_element_type=F32)
        own_scores = own_buf[pair * 2 : pair * 2 + 2].reshape(512, 128)
        top = jnp.max(
            jnp.maximum(jnp.maximum(prompt_scores[:, :128], prompt_scores[:, 128:]), own_scores), axis=1, keepdims=True
        )
        prompt_exp = jnp.exp2((prompt_scores - top) * (SCALE * LOG2E))
        own_exp = jnp.exp2((own_scores - top) * (SCALE * LOG2E))
        total = jnp.sum(prompt_exp[:, :128] + prompt_exp[:, 128:] + own_exp, axis=1, keepdims=True)
        factor = jnp.where(jnp.concatenate([live, live], axis=0), 1.0 / total, 0.0)
        mixed = jnp.dot(prompt_exp.astype(BF), latent[...], preferred_element_type=F32)
        own_weight = own_exp.reshape(2, 2, 128, 128)
        mixed_own = jnp.concatenate(
            [
                jnp.dot(
                    own_weight[:, half].reshape(256, 128).astype(BF),
                    fresh[half * 128 : (half + 1) * 128, :],
                    preferred_element_type=F32,
                ).reshape(2, 128, LAT)
                for half in range(2)
            ],
            axis=1,
        ).reshape(512, LAT)
        mixed = ((mixed + mixed_own) * factor).astype(BF)
        outs = []
        for sub in range(2):
            i = pair * 2 + sub
            out = jnp.dot(
                mixed[sub * TOK : (sub + 1) * TOK], vu[:, i * 128 : (i + 1) * 128], preferred_element_type=F32
            )
            outs.append(out.reshape(32, 8, 128))
        o_send[pair] = jnp.concatenate(outs, axis=1).astype(BF)

        for dz in z_order + (0,):
            for dy in (2, 1, 3, 0):
                if dy or dz:
                    there = lax.rem(y + dy, NY) * NZ + lax.rem(z + dz, NZ)
                    remote(
                        o_send.at[pair, there], out_ref.at[h, pair], o_ssem.at[pair], o_rsem.at[pair], (g, there)
                    ).start()

        keep = pltpu.make_async_copy(o_send.at[pair, h], out_ref.at[h, pair], local_sem.at[5 + pair])
        keep.start()

    for copy in w_out + wf_out + wc_out + k_out + q_out + qy_near + qy_far + qf_out + qf_far + kz_out + kf_out + p_out + pz_out + list(pg_out.values()) + py_out:
        copy.wait_send()
    for pair in range(2):
        pltpu.make_async_copy(o_send.at[pair, h], out_ref.at[h, pair], local_sem.at[5 + pair]).wait()
        whole = remote(
            o_send.at[pair, pl.ds(0, 31)], out_ref.at[pl.ds(0, 31), pair], o_ssem.at[pair], o_rsem.at[pair], sibling
        )
        whole.wait_send()
        whole.wait_recv()


def local(
    query_latent, response_keys, prompt_cache, owners, lengths, w_query_plain, w_query_rotary, w_key_up, w_value_up
):
    vmem = pl.BlockSpec(memory_space=pltpu.VMEM)
    hbm = pl.BlockSpec(memory_space=pltpu.HBM)
    dma = pltpu.SemaphoreType.DMA
    gathered = pl.pallas_call(
        kernel,
        out_shape=jax.ShapeDtypeStruct((32, 2, 16, 128), BF),
        in_specs=[hbm] * 10,
        out_specs=hbm,
        scratch_shapes=[
            pltpu.SMEM((1, 1), jnp.int32),
            pltpu.VMEM((8, QLAT), BF),
            pltpu.VMEM((8, 576), BF),
            pltpu.VMEM((1, 16), jnp.int32),
            pltpu.VMEM((32, 256), F32),
            pltpu.VMEM((QLAT, 768), BF),
            pltpu.VMEM((512, 512), BF),
            pltpu.VMEM((512, 512), BF),
            pltpu.VMEM((1, 147456), BF),
            pltpu.VMEM((PLEN, 512), F32),
            pltpu.VMEM((16, 768), BF),
            pltpu.VMEM((16, 256), BF),
            pltpu.VMEM((16, 128), BF),
            pltpu.VMEM((NY, NZ, 16, 768), BF),
            pltpu.VMEM((NY, NZ, 16, 256), BF),
            pltpu.VMEM((NY, 16, 128), BF),
            pltpu.VMEM((NZ, 16, 128), BF),
            pltpu.VMEM((NY, NZ, 16, 256), BF),
            pltpu.VMEM((NY, 2, 16, 128), BF),
            pltpu.VMEM((NY, NZ, 16, 256), BF),
            pltpu.VMEM((NY, 2, 16, 128), BF),
            pltpu.VMEM((NZ, 16, 384), BF),
            pltpu.VMEM((NZ, 16, 384), BF),
            pltpu.VMEM((NY, NZ, 16, 384), BF),
            pltpu.VMEM((TOK, QLAT), BF),
            pltpu.VMEM((TOK, 512), BF),
            pltpu.VMEM((TOK, 128), BF),
            pltpu.VMEM((PLEN, 512), BF),
            pltpu.VMEM((128, PLEN), BF),
            pltpu.VMEM((TOK, 512), BF),
            pltpu.VMEM((TOK, 256), BF),
            pltpu.VMEM((4, TOK, 512), BF),
            pltpu.VMEM((4, TOK, 128), F32),
            pltpu.VMEM((2, 32, 16, 128), BF),
            dma((12,)),
            *[dma((4, 2))] * 2,
            *[dma((2,))] * 2,
            *[dma((4, 2))] * 2,
            *[dma((8,))] * 2,
            *[dma((4, 3))] * 2,
            *[dma((4, 2))] * 2,
            *[dma((4, 2))] * 2,
            *[dma((8, 2))] * 2,
            *[dma((4, 2))] * 2,
            *[dma((8,))] * 4,
            *[dma((4, 4))] * 2,
            *[dma((2,))] * 2,
            pltpu.SemaphoreType.REGULAR,
        ],
        compiler_params=pltpu.CompilerParams(collective_id=0, has_side_effects=True, vmem_limit_bytes=60 << 20),
    )(
        owners.reshape(1, 1),
        query_latent,
        response_keys,
        lengths,
        jnp.asarray(rotary_tables()),
        prompt_cache,
        w_query_plain,
        w_query_rotary,
        w_key_up,
        w_value_up,
    )
    return gathered.reshape(32, 2, 2, 8, 128).transpose(3, 0, 1, 2, 4).reshape(8, 16384)


def solution(mesh):
    return jax.shard_map(
        local,
        mesh=mesh,
        in_specs=(
            P(("group", "head"), None),
            P(("group", "head"), None),
            P(("group", "head"), None),
            P("group"),
            P("group", None),
            P("group", "head"),
            P("group", "head"),
            P("head", None),
            P(None, "head"),
        ),
        out_specs=P(("group", "head"), None),
        check_vma=False,
    )
```

```python
import math

import jax
import jax.numpy as jnp
import numpy as np
from jax import lax
from jax.experimental import pallas as pl
from jax.experimental.pallas import tpu as pltpu
from jax.sharding import PartitionSpec as P

MESH = pl.DeviceIdType.MESH
LAT = 512
ROPE = 64
NOPE = 128
VDIM = 128
QLAT = 1536
PLEN = 256
RTOK = 16
TOK = 256
NX, NY, NZ = 4, 4, 8
SHARD = 192
HALF = 96
BF = jnp.bfloat16
F32 = jnp.float32
SCALE = 1.0 / math.sqrt(NOPE + ROPE)
LOG2E = 1.4426950408889634


def rotary_tables():
    position = (PLEN + np.arange(RTOK)).astype(np.float32)
    inverse = np.exp(np.arange(32).astype(np.float32) * np.float32(-2.0 * math.log(10000.0) / ROPE))
    angle = (position[:, None] * inverse[None, :].astype(np.float32)).astype(np.float32)
    cosine, sine = np.cos(angle), np.sin(angle)
    cos_table = np.tile(np.concatenate([cosine, cosine], 1), (1, 4))
    sin_table = np.tile(np.concatenate([-sine, sine], 1), (1, 4))
    return np.concatenate([cos_table, sin_table], 0).astype(np.float32)


def dot_nt(a, b):
    return lax.dot_general(a, b, (((1,), (1,)), ((), ())), preferred_element_type=F32)


def kernel(
    owner_hbm, query_hbm, keys_hbm, length_hbm, table_hbm, prompt_hbm, wp_hbm, wr_hbm, ku_hbm, vu_hbm,
    out_ref,
    owner_ref, query_ref, keys_ref, length_ref, table_ref, w, ku, vu, flat, stage, q_send, k_send, r_own, qb, kl, kt, kr,
    p_send, r_send, p_recv, r_recv, z_send, z_recv, pl_buf,
    x_buf, fresh, fresh_rot, latent, rotary, plain, turned, absorbed, own_buf, o_send,
    local_sem, wx_send, wx_recv, wf_send, wf_recv, wc_send, wc_recv,
    qz_send, qz_recv, qy_send, qy_recv, qf_send, qf_recv, ky_send, ky_recv, kz_send, kz_recv,
    pa_send, pa_recv, pz_send, pz_recv, pg_send, pg_recv, py_send, py_recv,
    o_ssem, o_rsem, ready,
):
    g = lax.axis_index("group")
    h = lax.axis_index("head")
    x, c = g // 2, g % 2
    y, z = h // NZ, h % NZ

    def at_x(d):
        return (lax.rem(x + d, NX) * 2 + c, h)

    def at_y(d):
        return (g, lax.rem(y + d, NY) * NZ + z)

    def at_z(d):
        return (g, y * NZ + lax.rem(z + d, NZ))

    sibling = (x * 2 + 1 - c, h)
    y_order = (1, 3, 2)
    z_far, z_near = (4, 3, 5), (2, 6, 1, 7)
    z_order = z_far + z_near

    def remote(src, dst, ssem, rsem, device):
        return pltpu.make_async_remote_copy(src, dst, ssem, rsem, device_id=device, device_id_type=MESH)

    barrier = pltpu.get_barrier_semaphore()
    peers = [sibling] + [at_x(d) for d in (1, 3)] + [at_y(d) for d in y_order] + [at_z(d) for d in z_near]
    for peer in peers:
        pl.semaphore_signal(barrier, inc=1, device_id=peer, device_id_type=MESH)

    def half_rows(dx, core, half):
        start = (lax.rem(x + dx + NX, NX) * 2 + core) * SHARD + half * HALF
        return pl.ds(pl.multiple_of(start, 32), HALF)

    mine = pl.ds(pl.multiple_of(g * SHARD, 64), SHARD)
    flat_copy = pltpu.make_async_copy(prompt_hbm, flat, local_sem.at[0])
    query_copy = pltpu.make_async_copy(query_hbm, query_ref, local_sem.at[7])
    keys_copy = pltpu.make_async_copy(keys_hbm, keys_ref, local_sem.at[8])
    wp_copy = pltpu.make_async_copy(wp_hbm, w.at[mine, 0:512], local_sem.at[3])
    wr_copy = pltpu.make_async_copy(wr_hbm, w.at[mine, 512:768], local_sem.at[4])
    owner_copy = pltpu.make_async_copy(owner_hbm, owner_ref, local_sem.at[9])
    length_copy = pltpu.make_async_copy(length_hbm, length_ref, local_sem.at[10])
    table_copy = pltpu.make_async_copy(table_hbm, table_ref, local_sem.at[11])
    ku_copy = pltpu.make_async_copy(ku_hbm, ku, local_sem.at[1])
    vu_copy = pltpu.make_async_copy(vu_hbm, vu, local_sem.at[2])
    for copy in (
        flat_copy, query_copy, keys_copy, wp_copy, wr_copy, owner_copy, length_copy, table_copy, ku_copy, vu_copy
    ):
        copy.start()

    flat_copy.wait()

    @pl.loop(0, PLEN // 8)
    def _(block):
        for r in range(8):
            row = flat[0:1, pl.ds(pl.multiple_of(block * 4096 + r * 512, 512), 512)].astype(F32)
            stage[pl.ds(block * 8 + r, 1), :] = row
        both = stage[pl.ds(pl.multiple_of(block * 8, 8), 8), :]
        p_send[pl.ds(block // 8, 1), pl.ds(block % 8, 1)] = jnp.concatenate(
            [both[:, :256], both[:, 256:]], axis=0
        ).astype(BF)[None, None]

    @pl.loop(0, NY)
    def _(j):
        for r in range(16):
            row = flat[0:1, pl.ds(pl.multiple_of(PLEN * LAT + j * 4096 + r * 256, 256), 256)].astype(F32)
            stage[pl.ds(r, 1), 0:256] = row
        both = stage[0:16, 0:256].astype(BF)
        r_send[pl.ds(j, 1), 0:1] = both[None, None, :, :128]
        r_send[pl.ds(j, 1), 1:2] = both[None, None, :, 128:]

    p_recv[pl.ds(y, 1)] = p_send[pl.ds(y, 1)]
    r_recv[pl.ds(y, 1)] = r_send[pl.ds(y, 1)]

    query_copy.wait()
    query = query_ref[...].astype(F32)
    packed = jnp.concatenate([query[:, :768], query[:, 768:]], axis=0).astype(BF)
    q_send[...] = packed
    qb[pl.ds(y, 1), 2:3] = packed[None, None]
    keys_copy.wait()
    keys = keys_ref[...].astype(F32)
    packed = jnp.concatenate([keys[:, :256], keys[:, 256:512]], axis=0).astype(BF)
    k_send[...] = packed
    kl[pl.ds(y, 1), pl.ds(z, 1)] = packed[None, None]
    rot = jnp.concatenate([keys[:, 512:], keys[:, 512:]], axis=1)
    packed = jnp.concatenate([rot, rot], axis=0).astype(BF)
    r_own[...] = packed
    kt[pl.ds(y, 1)] = packed[None]
    wp_copy.wait()
    wr_copy.wait()

    pl.semaphore_wait(barrier, len(peers))
    for d in (2, 6):
        pl.semaphore_signal(ready, inc=1, device_id=at_z(d), device_id_type=MESH)

    p_out, k_out = [], []
    for d in y_order:
        there = lax.rem(y + d, NY)
        k_out.append(remote(k_send, kl.at[y, z], ky_send.at[d, 0], ky_recv.at[d, 0], at_y(d)))
        k_out.append(remote(r_own, kt.at[y], ky_send.at[d, 1], ky_recv.at[d, 1], at_y(d)))
        p_out.append(remote(p_send.at[there], p_recv.at[y], pa_send.at[d, 0], pa_recv.at[d, 0], at_y(d)))
        p_out.append(remote(r_send.at[there], r_recv.at[y], pa_send.at[d, 1], pa_recv.at[d, 1], at_y(d)))
    q_out = [remote(q_send, qb.at[y, (10 - d) % NZ], qz_send.at[d], qz_recv.at[d], at_z(d)) for d in z_near + z_far]
    w_out = []
    for step in range(2):
        for d in (1, 3):
            half = step if d == 1 else 1 - step
            rows = w.at[half_rows(0, c, half)]
            w_out.append(remote(rows, rows, wx_send.at[d, half], wx_recv.at[d, half], at_x(d)))
    for copy in p_out + k_out + q_out[:4] + w_out:
        copy.start()
    wc_out = []

    def to_sibling(dx, half):
        rows = w.at[half_rows(dx, c, half)]
        wc_out.append(remote(rows, rows, wc_send.at[dx, half], wc_recv.at[dx, half], sibling))
        wc_out[-1].start()

    def from_sibling(dx, half):
        rows = w.at[half_rows(dx, 1 - c, half)]
        remote(rows, rows, wc_send.at[dx, half], wc_recv.at[dx, half], sibling).wait_recv()

    def arrived(d, half):
        rows = w.at[half_rows(NX - d, c, half)]
        remote(rows, rows, wx_send.at[d, half], wx_recv.at[d, half], at_x(d)).wait_recv()

    to_sibling(0, 0)
    to_sibling(0, 1)

    pl.semaphore_wait(ready, 2)
    for copy in q_out[4:]:
        copy.start()

    for copy in k_out:
        copy.wait_recv()
    tiles = kt[...].astype(F32)
    tile_row = lax.broadcasted_iota(jnp.int32, (16, 128), 0)
    tile_lane = lax.broadcasted_iota(jnp.int32, (16, 128), 1)
    upper = jnp.where(tile_lane < 64, tiles[0], tiles[1])
    lower = jnp.where(tile_lane < 64, tiles[2], tiles[3])
    kr[pl.ds(z, 1)] = jnp.where(tile_row < 8, upper, lower).astype(BF)[None]
    kz_out, kf_out = [], []

    def at(d):
        return lax.rem(z + d + NZ, NZ)

    def key_hop(copies, n, d, source, rows):
        part = kl.at[rows, at(source)]
        copies.append(remote(part, part, kz_send.at[n, 0], kz_recv.at[n, 0], at_z(d)))
        if n != 7:
            part = kr.at[at(source)]
            copies.append(remote(part, part, kz_send.at[n, 1], kz_recv.at[n, 1], at_z(d)))

    every = slice(0, NY)
    for n, d in enumerate((2, 6, 1, 7)):
        key_hop(kz_out, n, d, 0, every)
    key_hop(kf_out, 4, 6, 2, slice(0, 2))
    key_hop(kf_out, 7, 2, -2, slice(2, 4))
    key_hop(kf_out, 5, 1, -2, every)
    key_hop(kf_out, 6, 7, 2, every)

    wf_out = []

    def pass_on(d, half):
        arrived(d, half)
        rows = w.at[half_rows(NX - d, c, half)]
        wf_out.append(remote(rows, rows, wf_send.at[half], wf_recv.at[half], at_x(d)))
        wf_out[-1].start()
        to_sibling(NX - d, half)

    def query_hop(ssem, rsem, n, dy, first, last, d):
        part = qb.at[lax.rem(y + dy + NY, NY), first:last]
        return remote(part, part, ssem.at[d, n], rsem.at[d, n], at_y(d))

    for copy in q_out[:4]:
        copy.wait_recv()
    qy_near = [query_hop(qy_send, qy_recv, 0, 0, 0, 5, d) for d in (1, 3)]
    for copy in qy_near:
        copy.start()

    owner_copy.wait()
    owner = owner_ref[0, 0]
    for copy in p_out:
        copy.wait_recv()
    chosen = p_recv[owner // NZ]
    chosen_rot = r_recv[owner // NZ]
    for k in range(NZ):
        z_send[k] = jnp.concatenate([chosen[k], chosen_rot[k % 2]], axis=1)
    pz_out = []
    for d in z_order:
        pz_out.append(remote(z_send.at[lax.rem(z + d, NZ)], z_recv.at[z], pz_send.at[d], pz_recv.at[d], at_z(d)))
    for copy in pz_out:
        copy.start()
    z_recv[pl.ds(z, 1)] = z_send[pl.ds(z, 1)]

    pass_on(1, 0)
    pass_on(3, 1)

    for copy in q_out[4:]:
        copy.wait_recv()
    qy_far = [query_hop(qy_send, qy_recv, 1, 0, 5, 8, d) for d in (1, 3)]
    for copy in qy_far + kz_out:
        copy.start()
    for copy in qy_near:
        copy.wait_recv()
    qf_out = [query_hop(qf_send, qf_recv, 0, -1, 0, 3, 1), query_hop(qf_send, qf_recv, 0, 1, 3, 5, 3)]
    for copy in qf_out:
        copy.start()

    for copy in pz_out:
        copy.wait_recv()
    pl_buf[pl.ds(y, 1), 2:3] = z_recv[owner % NZ][None, None]
    pg_out = {}
    for d in z_order:
        pg_out[d] = remote(pl_buf.at[y, 2], pl_buf.at[y, (10 - d) % NZ], pg_send.at[d], pg_recv.at[d], at_z(d))
        pg_out[d].start()
    for copy in qy_far:
        copy.wait_recv()
    qf_far = [query_hop(qf_send, qf_recv, 1, 1, 6, 8, 3), query_hop(qf_send, qf_recv, 1, -1, 5, 6, 1)]
    for copy in qf_far:
        copy.start()
    for copy in kz_out:
        copy.wait_recv()
    for copy in kf_out:
        copy.start()
    arrived(1, 1)
    to_sibling(3, 1)
    arrived(3, 0)
    to_sibling(1, 0)
    for half in range(2):
        rows = w.at[half_rows(2, c, half)]
        remote(rows, rows, wf_send.at[half], wf_recv.at[half], sibling).wait_recv()
        to_sibling(2, half)

    py_out = []

    def spread_prompt(n, *index):
        part = pl_buf.at[(y, *index)]
        for d in y_order:
            py_out.append(remote(part, part, py_send.at[d, n], py_recv.at[d, n], at_y(d)))
            py_out[-1].start()

    for d in z_near:
        pg_out[d].wait_recv()
    spread_prompt(0, slice(0, 5), slice(None), slice(0, 256))
    spread_prompt(1, slice(2, 4), slice(None), slice(256, 384))
    for d in z_far:
        pg_out[d].wait_recv()
    spread_prompt(2, slice(5, 8), slice(None), slice(0, 256))

    for copy in qf_out + qf_far:
        copy.wait_recv()
    for j in range(NY):
        gathered = jnp.concatenate(
            [qb[pl.ds(j, 1), pl.ds(lax.rem(k - z + 10, NZ), 1)].astype(F32)[0] for k in range(NZ)], axis=0
        )
        x_buf[j * 64 : (j + 1) * 64, :768] = gathered[:, :8].reshape(64, 768).astype(BF)
        x_buf[j * 64 : (j + 1) * 64, 768:] = gathered[:, 8:].reshape(64, 768).astype(BF)
    for dx in range(NX):
        for half in range(2):
            from_sibling(dx, half)
    both = jnp.dot(x_buf[...], w[...], preferred_element_type=F32)
    plain[...] = both[:, :512].astype(BF)
    spun = both[:, 512:]
    lane = lax.broadcasted_iota(jnp.int32, (TOK, 256), 1)
    swapped = jnp.where(lane % 64 < 32, pltpu.roll(spun, 224, 1), pltpu.roll(spun, 32, 1))
    table_copy.wait()
    cosine = jnp.broadcast_to(table_ref[:16][None], (16, 16, 256)).reshape(TOK, 256)
    sine = jnp.broadcast_to(table_ref[16:][None], (16, 16, 256)).reshape(TOK, 256)
    turned[...] = (spun * cosine + swapped * sine).astype(BF)

    ku_copy.wait()
    for i in range(4):
        absorbed[i] = jnp.dot(
            plain[:, i * 128 : (i + 1) * 128], ku[i * 128 : (i + 1) * 128, :], preferred_element_type=F32
        ).astype(BF)

    for copy in kf_out:
        copy.wait_recv()
    gathered = kl[...].astype(F32).reshape(32, 16, 256)
    fresh[:, :256] = gathered[:, :8].reshape(TOK, 256).astype(BF)
    fresh[:, 256:] = gathered[:, 8:].reshape(TOK, 256).astype(BF)
    gathered = kr[...].astype(F32)
    rot_lane = lax.broadcasted_iota(jnp.int32, (64, 128), 1)
    for j in range(NY):
        piece = gathered[:, (j // 2) * 8 : (j // 2) * 8 + 8].reshape(64, 128)
        piece = jnp.where((rot_lane < 64) if j % 2 == 0 else (rot_lane >= 64), piece, 0.0)
        fresh_rot[j * 64 : (j + 1) * 64, :] = (piece + pltpu.roll(piece, 64, 1)).astype(BF)

    length_copy.wait()
    lengths = jnp.broadcast_to(length_ref[...], (TOK, 16))
    token = lax.broadcasted_iota(jnp.int32, (TOK, 16), 0)
    slot = lax.broadcasted_iota(jnp.int32, (TOK, 16), 1)
    limit = jnp.sum(jnp.where(token // RTOK == slot, lengths, 0).astype(F32), axis=1, keepdims=True)
    place = (lax.broadcasted_iota(jnp.int32, (TOK, 1), 0) % RTOK).astype(F32)
    live = place < limit

    t_half = lax.broadcasted_iota(jnp.int32, (128, 128), 0)
    s_half = lax.broadcasted_iota(jnp.int32, (128, 128), 1)
    allowed = (t_half // RTOK == s_half // RTOK) & (s_half <= t_half)
    pair_lane = lax.broadcasted_iota(jnp.int32, (TOK, 128), 1)

    def own_turned(i):
        mine_lanes = (pair_lane < 64) if i % 2 == 0 else (pair_lane >= 64)
        part = turned[:, (i // 2) * 128 : (i // 2 + 1) * 128].astype(F32)
        return jnp.where(mine_lanes, part, 0.0).astype(BF)

    for half in range(2):
        part = slice(half * 128, (half + 1) * 128)
        a = absorbed[:, part, :].reshape(512, LAT)
        t = jnp.concatenate([own_turned(i)[part] for i in range(4)], axis=0)
        scores = dot_nt(a, fresh[part, :]) + dot_nt(t, fresh_rot[part, :])
        own_buf[:, part, :] = jnp.where(allowed[None], scores.reshape(4, 128, 128), -jnp.inf)
    vu_copy.wait()

    for copy in py_out:
        copy.wait_recv()
    gathered = pl_buf[:, :, :, :256].astype(F32).reshape(32, 16, 256)
    latent[:, :256] = gathered[:, :8].reshape(PLEN, 256).astype(BF)
    latent[:, 256:] = gathered[:, 8:].reshape(PLEN, 256).astype(BF)
    tiles = []
    for j in range(NY):
        tiles.append(
            jnp.concatenate(
                [pl_buf[pl.ds(j, 1), pl.ds(2 + lax.rem(z + n, 2), 1), :, 256:].astype(F32)[0, 0] for n in range(2)], axis=1
            )
        )
    tiles = jnp.concatenate(tiles, axis=0)
    turn = lax.rem(z + 6, NZ) * 8
    key_lane = lax.broadcasted_iota(jnp.int32, (ROPE, PLEN), 1) % 64
    tiles = jnp.where(
        key_lane < 64 - turn, pltpu.roll(tiles, lax.rem(PLEN - turn, PLEN), 1), pltpu.roll(tiles, 64 - turn, 1)
    ).astype(BF)
    rotary[:64, :] = tiles
    rotary[64:, :] = tiles

    latent_t = latent[...].T
    for pair in range(2):
        a = absorbed[pair * 2 : pair * 2 + 2].reshape(512, LAT)
        t = jnp.concatenate([own_turned(pair * 2), own_turned(pair * 2 + 1)], axis=0)
        prompt_scores = jnp.dot(a, latent_t, preferred_element_type=F32) + jnp.dot(t, rotary[...], preferred_element_type=F32)
        own_scores = own_buf[pair * 2 : pair * 2 + 2].reshape(512, 128)
        top = jnp.max(
            jnp.maximum(jnp.maximum(prompt_scores[:, :128], prompt_scores[:, 128:]), own_scores), axis=1, keepdims=True
        )
        prompt_exp = jnp.exp2((prompt_scores - top) * (SCALE * LOG2E))
        own_exp = jnp.exp2((own_scores - top) * (SCALE * LOG2E))
        total = jnp.sum(prompt_exp[:, :128] + prompt_exp[:, 128:] + own_exp, axis=1, keepdims=True)
        factor = jnp.where(jnp.concatenate([live, live], axis=0), 1.0 / total, 0.0)
        mixed = jnp.dot(prompt_exp.astype(BF), latent[...], preferred_element_type=F32)
        own_weight = own_exp.reshape(2, 2, 128, 128)
        mixed_own = jnp.concatenate(
            [
                jnp.dot(
                    own_weight[:, half].reshape(256, 128).astype(BF),
                    fresh[half * 128 : (half + 1) * 128, :],
                    preferred_element_type=F32,
                ).reshape(2, 128, LAT)
                for half in range(2)
            ],
            axis=1,
        ).reshape(512, LAT)
        mixed = ((mixed + mixed_own) * factor).astype(BF)
        outs = []
        for sub in range(2):
            i = pair * 2 + sub
            out = jnp.dot(
                mixed[sub * TOK : (sub + 1) * TOK], vu[:, i * 128 : (i + 1) * 128], preferred_element_type=F32
            )
            outs.append(out.reshape(32, 8, 128))
        o_send[pair] = jnp.concatenate(outs, axis=1).astype(BF)

        for dz in z_order + (0,):
            for dy in (2, 1, 3, 0):
                if dy or dz:
                    there = lax.rem(y + dy, NY) * NZ + lax.rem(z + dz, NZ)
                    remote(
                        o_send.at[pair, there], out_ref.at[h, pair], o_ssem.at[pair], o_rsem.at[pair], (g, there)
                    ).start()

        keep = pltpu.make_async_copy(o_send.at[pair, h], out_ref.at[h, pair], local_sem.at[5 + pair])
        keep.start()

    for copy in w_out + wf_out + wc_out + k_out + q_out + qy_near + qy_far + qf_out + qf_far + kz_out + kf_out + p_out + pz_out + list(pg_out.values()) + py_out:
        copy.wait_send()
    for pair in range(2):
        pltpu.make_async_copy(o_send.at[pair, h], out_ref.at[h, pair], local_sem.at[5 + pair]).wait()
        whole = remote(
            o_send.at[pair, pl.ds(0, 31)], out_ref.at[pl.ds(0, 31), pair], o_ssem.at[pair], o_rsem.at[pair], sibling
        )
        whole.wait_send()
        whole.wait_recv()


def local(
    query_latent, response_keys, prompt_cache, owners, lengths, w_query_plain, w_query_rotary, w_key_up, w_value_up
):
    vmem = pl.BlockSpec(memory_space=pltpu.VMEM)
    hbm = pl.BlockSpec(memory_space=pltpu.HBM)
    dma = pltpu.SemaphoreType.DMA
    gathered = pl.pallas_call(
        kernel,
        out_shape=jax.ShapeDtypeStruct((32, 2, 16, 128), BF),
        in_specs=[hbm] * 10,
        out_specs=hbm,
        scratch_shapes=[
            pltpu.SMEM((1, 1), jnp.int32),
            pltpu.VMEM((8, QLAT), BF),
            pltpu.VMEM((8, 576), BF),
            pltpu.VMEM((1, 16), jnp.int32),
            pltpu.VMEM((32, 256), F32),
            pltpu.VMEM((QLAT, 768), BF),
            pltpu.VMEM((512, 512), BF),
            pltpu.VMEM((512, 512), BF),
            pltpu.VMEM((1, 147456), BF),
            pltpu.VMEM((PLEN, 512), F32),
            pltpu.VMEM((16, 768), BF),
            pltpu.VMEM((16, 256), BF),
            pltpu.VMEM((16, 128), BF),
            pltpu.VMEM((NY, NZ, 16, 768), BF),
            pltpu.VMEM((NY, NZ, 16, 256), BF),
            pltpu.VMEM((NY, 16, 128), BF),
            pltpu.VMEM((NZ, 16, 128), BF),
            pltpu.VMEM((NY, NZ, 16, 256), BF),
            pltpu.VMEM((NY, 2, 16, 128), BF),
            pltpu.VMEM((NY, NZ, 16, 256), BF),
            pltpu.VMEM((NY, 2, 16, 128), BF),
            pltpu.VMEM((NZ, 16, 384), BF),
            pltpu.VMEM((NZ, 16, 384), BF),
            pltpu.VMEM((NY, NZ, 16, 384), BF),
            pltpu.VMEM((TOK, QLAT), BF),
            pltpu.VMEM((TOK, 512), BF),
            pltpu.VMEM((TOK, 128), BF),
            pltpu.VMEM((PLEN, 512), BF),
            pltpu.VMEM((128, PLEN), BF),
            pltpu.VMEM((TOK, 512), BF),
            pltpu.VMEM((TOK, 256), BF),
            pltpu.VMEM((4, TOK, 512), BF),
            pltpu.VMEM((4, TOK, 128), F32),
            pltpu.VMEM((2, 32, 16, 128), BF),
            dma((12,)),
            *[dma((4, 2))] * 2,
            *[dma((2,))] * 2,
            *[dma((4, 2))] * 2,
            *[dma((8,))] * 2,
            *[dma((4, 3))] * 2,
            *[dma((4, 2))] * 2,
            *[dma((4, 2))] * 2,
            *[dma((8, 2))] * 2,
            *[dma((4, 2))] * 2,
            *[dma((8,))] * 4,
            *[dma((4, 4))] * 2,
            *[dma((2,))] * 2,
            pltpu.SemaphoreType.REGULAR,
        ],
        compiler_params=pltpu.CompilerParams(collective_id=0, has_side_effects=True, vmem_limit_bytes=60 << 20),
    )(
        owners.reshape(1, 1),
        query_latent,
        response_keys,
        lengths,
        jnp.asarray(rotary_tables()),
        prompt_cache,
        w_query_plain,
        w_query_rotary,
        w_key_up,
        w_value_up,
    )
    return gathered.reshape(32, 2, 2, 8, 128).transpose(3, 0, 1, 2, 4).reshape(8, 16384)


def solution(mesh):
    return jax.shard_map(
        local,
        mesh=mesh,
        in_specs=(
            P(("group", "head"), None),
            P(("group", "head"), None),
            P(("group", "head"), None),
            P("group"),
            P("group", None),
            P("group", "head"),
            P("group", "head"),
            P("head", None),
            P(None, "head"),
        ),
        out_specs=P(("group", "head"), None),
        check_vma=False,
    )
```
